512 devices in a mesh: section: 16 (over x_lo, y, core), seq: 32 (over x_hi, z).
Axes of the slice: x: 4 (x_hi: 2, x_lo: 2; x = x_hi * 2 + x_lo), y: 4, z: 16, core: 2. Of those that a mesh axis runs over, the one named last changes fastest.
Arguments:
- queries: bfloat16 [32768, 4096], P(('section', 'seq')), may hold values from -120 to 120
- keys: bfloat16 [32768, 4096], P(('section', 'seq')), may hold values from -6 to 6
- values: bfloat16 [32768, 4096], P(('section', 'seq')), may hold values from -6 to 6
- queue_state: bfloat16 [32768, 4096], P(('section', 'seq')), may hold values from -6 to 6
- fresh_state: bfloat16 [2048, 4096], P('seq'), may hold values from -6 to 6
- timestep: int32 [16], P('section'), may hold values from 1 to 15
- window_start: int32 [16, 2], P('section'), may hold values from -1 to 0, as said below
- modulation: float32 [16, 4096], replicated, may hold values from 0.1 to 1.9
Outputs:
- velocity: bfloat16 [32768, 4096], P(('section', 'seq'))
- advanced: bfloat16 [32768, 4096], P(('section', 'seq'))
The draws below stay inside these ranges and needn't reach their ends.
Inputs may be any that keep to these rules, and one draw needn't show every extreme that they name: `window_start`: each offset is -1 or 0.
All inputs are finite; a program needn't handle non-finite values.
Results may differ from the reference program's by a relative error of at most 0.0057.
Values may be sent and summed in bfloat16 or wider, within the bound.
No kernel may reach another device: no remote copies, remote signals or barrier semaphores. Data moves between devices by JAX's collectives and lax.ppermute only.
A program may use at most 64 MiB of HBM per device.

```python
import jax
import jax.numpy as jnp
from jax import lax

HEADS = 32
HEAD_DIM = 128
FRAMES = 2
NSTEPS = 16
FEAT = 4096
SECTION_TOK = 2048
FRAME_TOK = 1024
SECTIONS = 16
TOKENS = 32768


def shared_keys(key):
    return jnp.clip(jax.random.normal(key, (TOKENS, HEADS * HEAD_DIM), jnp.float32), -6.0, 6.0)


def draw_keys(key, part):
    base = shared_keys(key)
    return base.astype(jnp.bfloat16)


def draw_queries(key, part):
    key = jax.random.fold_in(key, 3)
    drawn = jnp.clip(jax.random.normal(key, (TOKENS, HEADS * HEAD_DIM), jnp.float32), -6.0, 6.0)
    return drawn.astype(jnp.bfloat16)


def draw_window_start(key, part):
    key = jax.random.fold_in(key, 11)
    drawn = jax.random.randint(key, (SECTIONS, FRAMES), -1, 1, dtype=jnp.int32)
    groups = jnp.arange(SECTIONS, dtype=jnp.int32)[:, None]
    frames = jnp.arange(FRAMES, dtype=jnp.int32)[None, :]
    forced = jnp.where(frames == 0, -1, 0).astype(jnp.int32)
    edge = (frames == 0) | (frames == FRAMES - 1)
    return jnp.where((groups % 2 == 1) & edge, forced, drawn).astype(jnp.int32)


def with_ends(values, stream_key, low, largest):
    longest = values.shape.index(max(values.shape))
    spots = []
    for shift in (0, 1):
        where = [jax.random.randint(jax.random.fold_in(stream_key, axis), (), 0, length) for axis, length in enumerate(values.shape)]
        where[longest] = (where[longest] + shift) % values.shape[longest]
        spots.append(tuple(where))
    return values.at[spots[0]].set(low).at[spots[1]].set(largest)


def levels(own_key, extent, cuts, smallest, high):
    loudness = 1.0
    for dim, parts in cuts:
        heights = jax.random.uniform(jax.random.fold_in(jax.random.fold_in(own_key, 6), dim), (parts,), jnp.float32, smallest / len(cuts), high / len(cuts))
        loudness = loudness * jnp.repeat(jnp.exp(heights), extent[dim] // parts).reshape((-1,) + (1,) * (len(extent) - 1 - dim))
    return loudness


def noise(stream_key, shape, spread, reach, cuts=(), kind=jnp.bfloat16):
    values = jax.random.normal(stream_key, shape, jnp.float32) * spread
    if len(cuts) > 0:
        values = levels(stream_key, shape, cuts, -0.22, 0.18) * values
    return jnp.clip(values, min=-reach, max=reach).astype(kind)


def setup_inputs(seed: int = 0) -> dict:
    arg_keys = jax.random.split(jax.random.key(seed), 9)
    return {
        "queries": draw_queries(jax.random.fold_in(arg_keys[8], 71), 0),
        "keys": draw_keys(jax.random.fold_in(arg_keys[8], 71), 0),
        "values": noise(arg_keys[2], (TOKENS, FEAT), 1.0, 6.0, ((0, 512),)),
        "queue_state": noise(arg_keys[3], (TOKENS, FEAT), 1.0, 6.0, ((0, 512),)),
        "fresh_state": noise(arg_keys[4], (SECTION_TOK, FEAT), 1.0, 6.0, ((0, 32),)),
        "timestep": with_ends(jax.random.randint(arg_keys[5], (SECTIONS,), 1, NSTEPS), jax.random.fold_in(arg_keys[5], 1), 1, NSTEPS - 1).astype(jnp.int32),
        "window_start": draw_window_start(jax.random.fold_in(arg_keys[8], 71), 0),
        "modulation": jnp.clip(1.0 + 0.18 * jax.random.normal(arg_keys[7], (NSTEPS, FEAT), jnp.float32), 0.1, 1.9),
    }


def level(step):
    share = step.astype(jnp.float32) / NSTEPS
    return 5.0 * share / (1.0 + 4.0 * share)

def attend(query_block, key_window, value_window, valid):
    scores = jnp.einsum('qhd,khd->hqk', query_block.astype(jnp.float32), key_window.astype(jnp.float32)) / jnp.sqrt(jnp.float32(HEAD_DIM))
    scores = jnp.where(valid[None, None, :], scores, -jnp.inf)
    peak = lax.optimization_barrier(jnp.max(scores, axis=-1, keepdims=True))
    expo = jnp.exp(scores - peak)
    total = lax.optimization_barrier(jnp.sum(expo, axis=-1))
    weights = expo.astype(jnp.bfloat16)
    mixed = jnp.einsum('hqk,khd->qhd', weights.astype(jnp.float32), value_window.astype(jnp.float32))
    return (mixed / jnp.transpose(total)[:, :, None]).astype(jnp.bfloat16)

def reference(queries, keys, values, queue_state, fresh_state, timestep, window_start, modulation):
    groups = TOKENS // SECTION_TOK
    shape4 = (groups, SECTION_TOK, HEADS, HEAD_DIM)
    query4 = queries.reshape(shape4)
    key4 = keys.reshape(shape4)
    value4 = values.reshape(shape4)
    state3 = queue_state.reshape(groups, SECTION_TOK, FEAT)

    def neighbours(array, group):
        before = lax.dynamic_index_in_dim(array, jnp.maximum(group - 1, 0), 0, keepdims=False)[SECTION_TOK - FRAME_TOK:]
        after = lax.dynamic_index_in_dim(array, jnp.minimum(group + 1, groups - 1), 0, keepdims=False)[:FRAME_TOK]
        before = jnp.where(group > 0, before, jnp.zeros_like(before))
        after = jnp.where(group < groups - 1, after, jnp.zeros_like(after))
        own = lax.dynamic_index_in_dim(array, group, 0, keepdims=False)
        return jnp.concatenate([before, own, after], axis=0)

    def one_group(group):
        extended_keys = neighbours(key4, group)
        extended_values = neighbours(value4, group)
        own_queries = lax.dynamic_index_in_dim(query4, group, 0, keepdims=False)
        pieces = []
        for frame in range(FRAMES):
            lead = frame + window_start[group, frame]
            first = ((lead + 1) * FRAME_TOK).astype(jnp.int32)
            key_window = lax.dynamic_slice_in_dim(extended_keys, first, 2 * FRAME_TOK, 0)
            value_window = lax.dynamic_slice_in_dim(extended_values, first, 2 * FRAME_TOK, 0)
            key_frame = lead + jnp.arange(2 * FRAME_TOK, dtype=jnp.int32) // FRAME_TOK
            valid = ((key_frame >= 0) | (group > 0)) & ((key_frame < FRAMES) | (group < groups - 1))
            pieces.append(attend(own_queries[frame * FRAME_TOK:(frame + 1) * FRAME_TOK], key_window, value_window, valid))
        attended = jnp.concatenate(pieces, axis=0).reshape(SECTION_TOK, FEAT).astype(jnp.float32)
        scale = jnp.sqrt(lax.optimization_barrier(jnp.mean(attended * attended, axis=-1, keepdims=True)) + 1e-06)
        step = timestep[group]
        gain = lax.dynamic_index_in_dim(modulation, step, 0, keepdims=False)
        moving = attended / scale * gain[None, :]
        delta = level(step - 1) - level(step)
        state = lax.dynamic_index_in_dim(state3, group, 0, keepdims=False).astype(jnp.float32)
        updated = (state + delta * moving).astype(jnp.bfloat16)
        return (moving.astype(jnp.bfloat16), updated)
    velocity, updated = lax.map(one_group, jnp.arange(groups, dtype=jnp.int32))
    advanced = jnp.concatenate([fresh_state[None], updated[:-1]], axis=0)
    return (velocity.reshape(TOKENS, FEAT), advanced.reshape(TOKENS, FEAT))
```

```python
import functools

import jax
import jax.numpy as jnp
from jax import lax
from jax.experimental import pallas as pl
from jax.experimental.pallas import tpu as pltpu
from jax.sharding import PartitionSpec as P

HEAD_DIM = 128
FRAMES = 2
NSTEPS = 16
LOG2E = 1.4426950408889634
VMEM = pl.BlockSpec(memory_space=pltpu.VMEM)
SMEM = pl.BlockSpec(memory_space=pltpu.SMEM)
BIG = 48 * 1024 * 1024


def level(step):
    share = step / NSTEPS
    return 5.0 * share / (1.0 + 4.0 * share)


def pack_kernel(q_ref, k_ref, v_ref, out_ref):
    for head in range(out_ref.shape[0]):
        cols = slice(head * HEAD_DIM, (head + 1) * HEAD_DIM)
        for part, ref in enumerate((q_ref, k_ref, v_ref)):
            out_ref[head, :, part * HEAD_DIM : (part + 1) * HEAD_DIM] = ref[:, cols]


def pack(queries, keys, values):
    tok, feat = queries.shape
    heads = feat // HEAD_DIM
    group = 8
    block = pl.BlockSpec((tok, group * HEAD_DIM), lambda i: (0, i))
    return pl.pallas_call(
        pack_kernel,
        grid=(heads // group,),
        in_specs=[block] * 3,
        out_specs=pl.BlockSpec((group, tok, 3 * HEAD_DIM), lambda i: (i, 0, 0)),
        out_shape=jax.ShapeDtypeStruct((heads, tok, 3 * HEAD_DIM), queries.dtype),
    )(queries, keys, values)


def attend_kernel(final, ws_ref, qkv_ref, before_ref, after_ref, out_ref, key_ref, value_ref):
    frame_tok = qkv_ref.shape[0] // FRAMES
    position = lax.axis_index("section")
    block = 256
    k_cols, v_cols = slice(HEAD_DIM, 2 * HEAD_DIM), slice(2 * HEAD_DIM, 3 * HEAD_DIM)
    ones = jnp.ones((2 * frame_tok, HEAD_DIM), jnp.bfloat16)
    value_ref[:, HEAD_DIM:] = ones

    def run(frame, length):
        keys, vals = key_ref[:length], value_ref[:length]
        for index in range(frame_tok // block):
            rows = pl.ds(frame * frame_tok + index * block, block)
            q = qkv_ref[rows, :HEAD_DIM]
            s = lax.dot_general(q, keys, (((1,), (1,)), ((), ())), preferred_element_type=jnp.float32)
            peak = jnp.max(s, axis=-1, keepdims=True)
            w = jnp.exp2((s - peak) * (LOG2E / HEAD_DIM**0.5)).astype(jnp.bfloat16)
            mixed = jnp.dot(w, vals, preferred_element_type=jnp.float32)
            out_ref[rows, :] = (mixed[:, :HEAD_DIM] / mixed[:, HEAD_DIM:]).astype(jnp.bfloat16)

    for frame in range(FRAMES):
        own = pl.ds(frame * frame_tok, frame_tok)
        key_ref[:frame_tok] = qkv_ref[own, k_cols]
        value_ref[:frame_tok, :HEAD_DIM] = qkv_ref[own, v_cols]
        start = ws_ref[0, frame]
        outside = (start == -1) if frame == 0 else (start == 0)
        halo = before_ref if frame == 0 else after_ref
        exists = (position > 0) if frame == 0 else (position < final)

        @pl.when(outside)
        def _():
            key_ref[frame_tok:] = halo[:, :HEAD_DIM]
            value_ref[frame_tok:, :HEAD_DIM] = halo[:, HEAD_DIM:]

        @pl.when(jnp.logical_not(outside))
        def _():
            other = pl.ds((1 - frame) * frame_tok, frame_tok)
            key_ref[frame_tok:] = qkv_ref[other, k_cols]
            value_ref[frame_tok:, :HEAD_DIM] = qkv_ref[other, v_cols]

        both = jnp.logical_or(jnp.logical_not(outside), exists)
        pl.when(both)(functools.partial(run, frame, 2 * frame_tok))
        pl.when(jnp.logical_not(both))(functools.partial(run, frame, frame_tok))


def attend(window_start, qkv, before, after, final):
    tok = qkv.shape[0]
    return pl.pallas_call(
        functools.partial(attend_kernel, final),
        in_specs=[SMEM, VMEM, VMEM, VMEM],
        out_specs=VMEM,
        out_shape=jax.ShapeDtypeStruct((tok, HEAD_DIM), qkv.dtype),
        scratch_shapes=[
            pltpu.VMEM((tok, HEAD_DIM), jnp.bfloat16),
            pltpu.VMEM((tok, 2 * HEAD_DIM), jnp.bfloat16),
        ],
        compiler_params=pltpu.CompilerParams(vmem_limit_bytes=BIG),
    )(window_start, qkv, before, after)


def finish_kernel(final, step_ref, att_ref, state_ref, fresh_ref, mod_ref, velocity_ref, passed_ref):
    heads, tok, _ = att_ref.shape
    position = lax.axis_index("section")
    step = step_ref[0]
    squares = jnp.zeros((tok, HEAD_DIM), jnp.float32)
    for head in range(heads):
        a = att_ref[head].astype(jnp.float32)
        squares += a * a
    mean = jnp.sum(squares, axis=-1, keepdims=True) / (heads * HEAD_DIM)
    scale = jnp.sqrt(mean + 1e-06)
    inverse = jnp.broadcast_to(1.0 / scale, (tok, HEAD_DIM))
    now = jnp.full((1, HEAD_DIM), step, jnp.int32)
    delta = level((now - 1).astype(jnp.float32)) - level(now.astype(jnp.float32))
    delta = jnp.broadcast_to(delta, (tok, HEAD_DIM))
    chosen = lax.broadcasted_iota(jnp.int32, (NSTEPS, HEAD_DIM), 0) == step
    for head in range(heads):
        cols = slice(head * HEAD_DIM, (head + 1) * HEAD_DIM)
        gain = jnp.sum(jnp.where(chosen, mod_ref[:, cols], 0.0), axis=0, keepdims=True)
        moving = att_ref[head].astype(jnp.float32) * inverse * gain
        velocity_ref[:, cols] = moving.astype(jnp.bfloat16)
        updated = state_ref[:, cols].astype(jnp.float32) + delta * moving
        passed_ref[:, cols] = updated.astype(jnp.bfloat16)

    @pl.when(position == final)
    def _():
        passed_ref[...] = fresh_ref[...]


def finish(timestep, attended, state, fresh, modulation, final):
    return pl.pallas_call(
        functools.partial(finish_kernel, final),
        in_specs=[SMEM, VMEM, VMEM, VMEM, VMEM],
        out_specs=[VMEM, VMEM],
        out_shape=[jax.ShapeDtypeStruct(state.shape, state.dtype)] * 2,
        compiler_params=pltpu.CompilerParams(vmem_limit_bytes=BIG),
    )(timestep, attended, state, fresh, modulation)


def per_device(queries, keys, values, queue_state, fresh_state, timestep, window_start, modulation):
    tok_dev, feat = queries.shape
    sections = lax.axis_size("section")
    frame_tok = tok_dev * lax.axis_size("seq") // FRAMES
    packed = pack(queries, keys, values)
    qkv = lax.all_to_all(packed, "seq", split_axis=0, concat_axis=0, tiled=True)
    qkv = qkv.reshape(FRAMES * frame_tok, 3 * HEAD_DIM)
    up = [(i, i + 1) for i in range(sections - 1)]
    down = [(j, i) for i, j in up]
    before = lax.ppermute(qkv[frame_tok:, HEAD_DIM:], "section", up)
    after = lax.ppermute(qkv[:frame_tok, HEAD_DIM:], "section", down)
    attended = attend(window_start, qkv, before, after, sections - 1)
    attended = attended.reshape(feat // HEAD_DIM, tok_dev, HEAD_DIM)
    attended = lax.all_to_all(attended, "seq", split_axis=0, concat_axis=0, tiled=True)
    velocity, passed = finish(timestep, attended, queue_state, fresh_state, modulation, sections - 1)
    ring = [(i, (i + 1) % sections) for i in range(sections)]
    return velocity, lax.ppermute(passed, "section", ring)


def solution(mesh):
    return jax.shard_map(
        per_device,
        mesh=mesh,
        in_specs=(
            P(("section", "seq"), None),
            P(("section", "seq"), None),
            P(("section", "seq"), None),
            P(("section", "seq"), None),
            P("seq", None),
            P("section"),
            P("section", None),
            P(),
        ),
        out_specs=(P(("section", "seq"), None), P(("section", "seq"), None)),
        check_vma=False,
    )
```

```python
import functools

import jax
import jax.numpy as jnp
from jax import lax
from jax.experimental import pallas as pl
from jax.experimental.pallas import tpu as pltpu
from jax.sharding import PartitionSpec as P

HEAD_DIM = 128
FRAMES = 2
NSTEPS = 16
SCALE = 1.4426950408889634 / HEAD_DIM**0.5
BLOCK = 256
VMEM = pl.BlockSpec(memory_space=pltpu.VMEM)
SMEM = pl.BlockSpec(memory_space=pltpu.SMEM)
LIMIT = 24 * 1024 * 1024


def level(step):
    share = step / NSTEPS
    return 5.0 * share / (1.0 + 4.0 * share)


def pack_kernel(q_ref, k_ref, v_ref, out_ref):
    for head in range(out_ref.shape[0]):
        cols = slice(head * HEAD_DIM, (head + 1) * HEAD_DIM)
        for part, ref in enumerate((q_ref, k_ref, v_ref)):
            out_ref[head, :, part * HEAD_DIM : (part + 1) * HEAD_DIM] = ref[:, cols]


def pack(queries, keys, values):
    tok, feat = queries.shape
    heads = feat // HEAD_DIM
    return pl.pallas_call(
        pack_kernel,
        in_specs=[VMEM] * 3,
        out_specs=VMEM,
        out_shape=jax.ShapeDtypeStruct((heads, tok, 3 * HEAD_DIM), queries.dtype),
        compiler_params=pltpu.CompilerParams(vmem_limit_bytes=LIMIT),
    )(queries, keys, values)


def scores_of(q, keys):
    return lax.dot_general(q, keys, (((1,), (1,)), ((), ())), preferred_element_type=jnp.float32)


def own_kernel(qkv_ref, sums_ref, peak_ref, value_ref):
    frame_tok = qkv_ref.shape[0] // FRAMES
    value_ref[:, :HEAD_DIM] = qkv_ref[:, 2 * HEAD_DIM :]
    value_ref[:, HEAD_DIM:] = jnp.ones((FRAMES * frame_tok, HEAD_DIM), jnp.bfloat16)
    for frame in range(FRAMES):
        own = pl.ds(frame * frame_tok, frame_tok)
        for index in range(frame_tok // BLOCK):
            rows = pl.ds(frame * frame_tok + index * BLOCK, BLOCK)
            scores = scores_of(qkv_ref[rows, :HEAD_DIM], qkv_ref[own, HEAD_DIM : 2 * HEAD_DIM])
            peak = jnp.max(scores, axis=-1, keepdims=True)
            weights = jnp.exp2((scores - peak) * SCALE).astype(jnp.bfloat16)
            sums_ref[rows, :] = jnp.dot(weights, value_ref[own, :], preferred_element_type=jnp.float32)
            peak_ref[rows, :] = jnp.broadcast_to(peak, (BLOCK, HEAD_DIM))


def own_part(qkv):
    tok = qkv.shape[0]
    return pl.pallas_call(
        own_kernel,
        in_specs=[VMEM],
        out_specs=[VMEM, VMEM],
        out_shape=[
            jax.ShapeDtypeStruct((tok, 2 * HEAD_DIM), jnp.float32),
            jax.ShapeDtypeStruct((tok, HEAD_DIM), jnp.float32),
        ],
        scratch_shapes=[pltpu.VMEM((tok, 2 * HEAD_DIM), jnp.bfloat16)],
        compiler_params=pltpu.CompilerParams(vmem_limit_bytes=LIMIT),
        cost_estimate=pl.CostEstimate(
            flops=6 * tok * tok // FRAMES * HEAD_DIM,
            bytes_accessed=10 * tok * HEAD_DIM,
            transcendentals=tok * tok // FRAMES,
        ),
    )(qkv)


def other_kernel(final, ws_ref, qkv_ref, near_ref, far_ref, sums_ref, peak_ref, out_ref, key_ref, value_ref):
    frame_tok = qkv_ref.shape[0] // FRAMES
    position = lax.axis_index("section")
    odd = lax.rem(position, 2) == 1
    k_cols, v_cols = slice(HEAD_DIM, 2 * HEAD_DIM), slice(2 * HEAD_DIM, 3 * HEAD_DIM)
    for frame in range(FRAMES):
        start = ws_ref[0, frame]
        outside = (start == -1) if frame == 0 else (start == 0)
        exists = (position > 0) if frame == 0 else (position < final)
        by_near = odd if frame == 0 else jnp.logical_not(odd)
        own = pl.ds(frame * frame_tok, frame_tok)
        other = pl.ds((1 - frame) * frame_tok, frame_tok)

        @pl.when(jnp.logical_not(outside))
        def _():
            key_ref[frame] = qkv_ref[other, k_cols]
            value_ref[frame, :, :HEAD_DIM] = qkv_ref[other, v_cols]

        for ref, chosen in ((near_ref, by_near), (far_ref, jnp.logical_not(by_near))):

            @pl.when(jnp.logical_and(outside, jnp.logical_and(exists, chosen)))
            def _():
                key_ref[frame] = ref[:, :HEAD_DIM]
                value_ref[frame, :, :HEAD_DIM] = ref[:, HEAD_DIM:]

        missing = jnp.logical_and(outside, jnp.logical_not(exists))

        @pl.when(jnp.logical_not(missing))
        def _():
            value_ref[frame, :, HEAD_DIM:] = jnp.ones((frame_tok, HEAD_DIM), jnp.bfloat16)

        @pl.when(missing)
        def _():
            key_ref[frame] = qkv_ref[own, k_cols]
            value_ref[frame] = jnp.zeros((frame_tok, 2 * HEAD_DIM), jnp.bfloat16)

    for frame in range(FRAMES):
        for index in range(frame_tok // BLOCK):
            rows = pl.ds(frame * frame_tok + index * BLOCK, BLOCK)
            scores = scores_of(qkv_ref[rows, :HEAD_DIM], key_ref[frame])
            before = peak_ref[rows, :]
            peak = jnp.maximum(jnp.max(scores, axis=-1, keepdims=True), before[:, :1])
            weights = jnp.exp2((scores - peak) * SCALE).astype(jnp.bfloat16)
            sums = jnp.dot(weights, value_ref[frame], preferred_element_type=jnp.float32)
            share = jnp.exp2((before - peak) * SCALE)
            mixed = sums[:, :HEAD_DIM] + sums_ref[rows, :HEAD_DIM] * share
            total = sums[:, HEAD_DIM:] + sums_ref[rows, HEAD_DIM:] * share
            out_ref[rows, :] = (mixed / total).astype(jnp.bfloat16)


def other_part(window_start, qkv, near, far, sums, peak, final):
    tok = qkv.shape[0]
    return pl.pallas_call(
        functools.partial(other_kernel, final),
        in_specs=[SMEM] + [VMEM] * 5,
        out_specs=VMEM,
        out_shape=jax.ShapeDtypeStruct((tok, HEAD_DIM), qkv.dtype),
        scratch_shapes=[
            pltpu.VMEM((FRAMES, tok // FRAMES, HEAD_DIM), jnp.bfloat16),
            pltpu.VMEM((FRAMES, tok // FRAMES, 2 * HEAD_DIM), jnp.bfloat16),
        ],
        compiler_params=pltpu.CompilerParams(vmem_limit_bytes=LIMIT),
    )(window_start, qkv, near, far, sums, peak)


def finish_kernel(final, step_ref, att_ref, state_ref, fresh_ref, mod_ref, velocity_ref, passed_ref):
    heads, tok, _ = att_ref.shape
    position = lax.axis_index("section")
    step = step_ref[0]
    squares = jnp.zeros((tok, HEAD_DIM), jnp.float32)
    for head in range(heads):
        a = att_ref[head].astype(jnp.float32)
        squares += a * a
    mean = jnp.sum(squares, axis=-1, keepdims=True) / (heads * HEAD_DIM)
    scale = jnp.sqrt(mean + 1e-06)
    inverse = jnp.broadcast_to(1.0 / scale, (tok, HEAD_DIM))
    now = jnp.full((1, HEAD_DIM), step, jnp.int32)
    delta = level((now - 1).astype(jnp.float32)) - level(now.astype(jnp.float32))
    delta = jnp.broadcast_to(delta, (tok, HEAD_DIM))
    chosen = lax.broadcasted_iota(jnp.int32, (NSTEPS, HEAD_DIM), 0) == step
    for head in range(heads):
        cols = slice(head * HEAD_DIM, (head + 1) * HEAD_DIM)
        gain = jnp.sum(jnp.where(chosen, mod_ref[:, cols], 0.0), axis=0, keepdims=True)
        moving = att_ref[head].astype(jnp.float32) * inverse * gain
        velocity_ref[:, cols] = moving.astype(jnp.bfloat16)
        updated = state_ref[:, cols].astype(jnp.float32) + delta * moving
        passed_ref[:, cols] = updated.astype(jnp.bfloat16)

    @pl.when(position == final)
    def _():
        passed_ref[...] = fresh_ref[...]


def finish(timestep, attended, state, fresh, modulation, final):
    return pl.pallas_call(
        functools.partial(finish_kernel, final),
        in_specs=[SMEM, VMEM, VMEM, VMEM, VMEM],
        out_specs=[VMEM, VMEM],
        out_shape=[jax.ShapeDtypeStruct(state.shape, state.dtype)] * 2,
        compiler_params=pltpu.CompilerParams(vmem_limit_bytes=LIMIT),
    )(timestep, attended, state, fresh, modulation)


def per_device(queries, keys, values, queue_state, fresh_state, timestep, window_start, modulation):
    tok_dev, feat = queries.shape
    sections = lax.axis_size("section")
    frame_tok = tok_dev * lax.axis_size("seq") // FRAMES
    packed = pack(queries, keys, values)
    qkv = lax.all_to_all(packed, "seq", split_axis=0, concat_axis=0, tiled=True)
    qkv = qkv.reshape(FRAMES * frame_tok, 3 * HEAD_DIM)
    odd = lax.rem(lax.axis_index("section"), 2)
    facing = [lax.dynamic_slice(qkv, (f * frame_tok, HEAD_DIM), (frame_tok, 2 * HEAD_DIM)) for f in (odd, 1 - odd)]
    pairs = [(i, i + 1) for i in range(1, sections - 1, 2)]
    far = lax.ppermute(facing[0], "section", pairs + [(j, i) for i, j in pairs])
    pairs = [(i, i + 1) for i in range(0, sections - 1, 2)]
    near = lax.ppermute(facing[1], "section", pairs + [(j, i) for i, j in pairs])
    sums, peak = own_part(qkv)
    attended = other_part(window_start, qkv, near, far, sums, peak, sections - 1)
    attended = attended.reshape(feat // HEAD_DIM, tok_dev, HEAD_DIM)
    attended = lax.all_to_all(attended, "seq", split_axis=0, concat_axis=0, tiled=True)
    velocity, passed = finish(timestep, attended, queue_state, fresh_state, modulation, sections - 1)
    ring = [(i, (i + 1) % sections) for i in range(sections)]
    return velocity, lax.ppermute(passed, "section", ring)


def solution(mesh):
    return jax.shard_map(
        per_device,
        mesh=mesh,
        in_specs=(
            P(("section", "seq"), None),
            P(("section", "seq"), None),
            P(("section", "seq"), None),
            P(("section", "seq"), None),
            P("seq", None),
            P("section"),
            P("section", None),
            P(),
        ),
        out_specs=(P(("section", "seq"), None), P(("section", "seq"), None)),
        check_vma=False,
    )
```

```python
import functools

import jax
import jax.numpy as jnp
from jax import lax
from jax.experimental import pallas as pl
from jax.experimental.pallas import tpu as pltpu
from jax.sharding import PartitionSpec as P

HEAD_DIM = 128
FRAMES = 2
NSTEPS = 16
SCALE = 1.4426950408889634 / HEAD_DIM**0.5
BLOCK = 256
CHUNKS = 4
VMEM = pl.BlockSpec(memory_space=pltpu.VMEM)
HBM = pl.BlockSpec(memory_space=pltpu.HBM)
SMEM = pl.BlockSpec(memory_space=pltpu.SMEM)
LIMIT = 24 * 1024 * 1024
WHOLE = 63 * 1024 * 1024


def level(step):
    share = step / NSTEPS
    return 5.0 * share / (1.0 + 4.0 * share)


def pack_kernel(q_ref, k_ref, v_ref, out_ref, held_ref, packed_ref, in_sem, out_sem):
    heads = out_ref.shape[0]
    group = heads // CHUNKS
    copies = []
    for chunk in range(CHUNKS):
        cols = slice(chunk * group * HEAD_DIM, (chunk + 1) * group * HEAD_DIM)
        for part, ref in enumerate((q_ref, k_ref, v_ref)):
            copy = pltpu.make_async_copy(ref.at[:, cols], held_ref.at[part, :, cols], in_sem.at[chunk, part])
            copy.start()
            copies.append(copy)
    for chunk in range(CHUNKS):
        mine = slice(chunk * group, (chunk + 1) * group)
        for part in range(3):
            copies[3 * chunk + part].wait()
            for head in range(chunk * group, (chunk + 1) * group):
                cols = slice(head * HEAD_DIM, (head + 1) * HEAD_DIM)
                packed_ref[head, :, part * HEAD_DIM : (part + 1) * HEAD_DIM] = held_ref[part, :, cols]
        copy = pltpu.make_async_copy(packed_ref.at[mine], out_ref.at[mine], out_sem.at[chunk])
        copy.start()
        copies.append(copy)
    for copy in copies[3 * CHUNKS :]:
        copy.wait()


def pack(queries, keys, values):
    tok, feat = queries.shape
    heads = feat // HEAD_DIM
    shape = (heads, tok, 3 * HEAD_DIM)
    return pl.pallas_call(
        pack_kernel,
        in_specs=[HBM] * 3,
        out_specs=HBM,
        out_shape=jax.ShapeDtypeStruct(shape, queries.dtype),
        scratch_shapes=[
            pltpu.VMEM((3, tok, feat), queries.dtype),
            pltpu.VMEM(shape, queries.dtype),
            pltpu.SemaphoreType.DMA((CHUNKS, 3)),
            pltpu.SemaphoreType.DMA((CHUNKS,)),
        ],
        compiler_params=pltpu.CompilerParams(vmem_limit_bytes=WHOLE),
    )(queries, keys, values)


def scores_of(q, keys):
    return lax.dot_general(q, keys, (((1,), (1,)), ((), ())), preferred_element_type=jnp.float32)


def own_kernel(qkv_ref, sums_ref, peak_ref, value_ref):
    frame_tok = qkv_ref.shape[0] // FRAMES
    value_ref[:, :HEAD_DIM] = qkv_ref[:, 2 * HEAD_DIM :]
    value_ref[:, HEAD_DIM:] = jnp.ones((FRAMES * frame_tok, HEAD_DIM), jnp.bfloat16)
    for frame in range(FRAMES):
        own = pl.ds(frame * frame_tok, frame_tok)
        for index in range(frame_tok // BLOCK):
            rows = pl.ds(frame * frame_tok + index * BLOCK, BLOCK)
            scores = scores_of(qkv_ref[rows, :HEAD_DIM], qkv_ref[own, HEAD_DIM : 2 * HEAD_DIM])
            peak = jnp.max(scores, axis=-1, keepdims=True)
            weights = jnp.exp2((scores - peak) * SCALE).astype(jnp.bfloat16)
            sums_ref[rows, :] = jnp.dot(weights, value_ref[own, :], preferred_element_type=jnp.float32)
            peak_ref[rows, :] = jnp.broadcast_to(peak, (BLOCK, HEAD_DIM))


def own_part(qkv):
    tok = qkv.shape[0]
    return pl.pallas_call(
        own_kernel,
        in_specs=[VMEM],
        out_specs=[VMEM, VMEM],
        out_shape=[
            jax.ShapeDtypeStruct((tok, 2 * HEAD_DIM), jnp.float32),
            jax.ShapeDtypeStruct((tok, HEAD_DIM), jnp.float32),
        ],
        scratch_shapes=[pltpu.VMEM((tok, 2 * HEAD_DIM), jnp.bfloat16)],
        compiler_params=pltpu.CompilerParams(vmem_limit_bytes=LIMIT),
        cost_estimate=pl.CostEstimate(
            flops=6 * tok * tok // FRAMES * HEAD_DIM,
            bytes_accessed=10 * tok * HEAD_DIM,
            transcendentals=tok * tok // FRAMES,
        ),
    )(qkv)


def other_kernel(final, ws_ref, qkv_ref, far_ref, near_ref, sums_ref, peak_ref, out_ref, key_ref, value_ref):
    frame_tok = qkv_ref.shape[0] // FRAMES
    position = lax.axis_index("section")
    odd = lax.rem(position, 2) == 1
    k_cols, v_cols = slice(HEAD_DIM, 2 * HEAD_DIM), slice(2 * HEAD_DIM, 3 * HEAD_DIM)
    for frame in range(FRAMES):
        start = ws_ref[0, frame]
        outside = (start == -1) if frame == 0 else (start == 0)
        exists = (position > 0) if frame == 0 else (position < final)
        by_near = odd if frame == 0 else jnp.logical_not(odd)
        own = pl.ds(frame * frame_tok, frame_tok)
        other = pl.ds((1 - frame) * frame_tok, frame_tok)

        @pl.when(jnp.logical_not(outside))
        def _():
            key_ref[frame] = qkv_ref[other, k_cols]
            value_ref[frame, :, :HEAD_DIM] = qkv_ref[other, v_cols]

        for ref, chosen in ((near_ref, by_near), (far_ref, jnp.logical_not(by_near))):

            @pl.when(jnp.logical_and(outside, jnp.logical_and(exists, chosen)))
            def _():
                key_ref[frame] = ref[:, :HEAD_DIM]
                value_ref[frame, :, :HEAD_DIM] = ref[:, HEAD_DIM:]

        missing = jnp.logical_and(outside, jnp.logical_not(exists))

        @pl.when(jnp.logical_not(missing))
        def _():
            value_ref[frame, :, HEAD_DIM:] = jnp.ones((frame_tok, HEAD_DIM), jnp.bfloat16)

        @pl.when(missing)
        def _():
            key_ref[frame] = qkv_ref[own, k_cols]
            value_ref[frame] = jnp.zeros((frame_tok, 2 * HEAD_DIM), jnp.bfloat16)

    for frame in range(FRAMES):
        for index in range(frame_tok // BLOCK):
            rows = pl.ds(frame * frame_tok + index * BLOCK, BLOCK)
            scores = scores_of(qkv_ref[rows, :HEAD_DIM], key_ref[frame])
            before = peak_ref[rows, :]
            peak = jnp.maximum(jnp.max(scores, axis=-1, keepdims=True), before[:, :1])
            weights = jnp.exp2((scores - peak) * SCALE).astype(jnp.bfloat16)
            sums = jnp.dot(weights, value_ref[frame], preferred_element_type=jnp.float32)
            share = jnp.exp2((before - peak) * SCALE)
            mixed = sums[:, :HEAD_DIM] + sums_ref[rows, :HEAD_DIM] * share
            total = sums[:, HEAD_DIM:] + sums_ref[rows, HEAD_DIM:] * share
            out_ref[rows, :] = (mixed / total).astype(jnp.bfloat16)


def other_part(window_start, qkv, far, near, sums, peak, final):
    tok = qkv.shape[0]
    return pl.pallas_call(
        functools.partial(other_kernel, final),
        in_specs=[SMEM] + [VMEM] * 5,
        out_specs=VMEM,
        out_shape=jax.ShapeDtypeStruct((tok, HEAD_DIM), qkv.dtype),
        scratch_shapes=[
            pltpu.VMEM((FRAMES, tok // FRAMES, HEAD_DIM), jnp.bfloat16),
            pltpu.VMEM((FRAMES, tok // FRAMES, 2 * HEAD_DIM), jnp.bfloat16),
        ],
        compiler_params=pltpu.CompilerParams(vmem_limit_bytes=LIMIT),
    )(window_start, qkv, far, near, sums, peak)


def velocity_of(step_ref, att_ref, mod_ref):
    heads, tok, _ = att_ref.shape
    squares = jnp.zeros((tok, HEAD_DIM), jnp.float32)
    for head in range(heads):
        a = att_ref[head].astype(jnp.float32)
        squares += a * a
    mean = jnp.sum(squares, axis=-1, keepdims=True) / (heads * HEAD_DIM)
    inverse = jnp.broadcast_to(1.0 / jnp.sqrt(mean + 1e-06), (tok, HEAD_DIM))
    chosen = lax.broadcasted_iota(jnp.int32, (NSTEPS, HEAD_DIM), 0) == step_ref[0]
    for head in range(heads):
        cols = slice(head * HEAD_DIM, (head + 1) * HEAD_DIM)
        gain = jnp.sum(jnp.where(chosen, mod_ref[:, cols], 0.0), axis=0, keepdims=True)
        yield cols, att_ref[head].astype(jnp.float32) * inverse * gain


def update_kernel(final, step_ref, att_ref, mod_ref, state_ref, fresh_ref, passed_ref):
    now = jnp.full((1, HEAD_DIM), step_ref[0], jnp.int32)
    delta = level((now - 1).astype(jnp.float32)) - level(now.astype(jnp.float32))
    for cols, moving in velocity_of(step_ref, att_ref, mod_ref):
        passed_ref[:, cols] = (state_ref[:, cols].astype(jnp.float32) + delta * moving).astype(jnp.bfloat16)

    @pl.when(lax.axis_index("section") == final)
    def _():
        passed_ref[...] = fresh_ref[...]


def velocity_kernel(step_ref, att_ref, mod_ref, velocity_ref):
    for cols, moving in velocity_of(step_ref, att_ref, mod_ref):
        velocity_ref[:, cols] = moving.astype(jnp.bfloat16)


def finish(kernel, timestep, attended, modulation, *others):
    heads, tok, _ = attended.shape
    return pl.pallas_call(
        kernel,
        in_specs=[SMEM] + [VMEM] * (2 + len(others)),
        out_specs=VMEM,
        out_shape=jax.ShapeDtypeStruct((tok, heads * HEAD_DIM), attended.dtype),
        compiler_params=pltpu.CompilerParams(vmem_limit_bytes=LIMIT),
        cost_estimate=pl.CostEstimate(flops=10 * tok * heads * HEAD_DIM, bytes_accessed=6 * tok * heads * HEAD_DIM, transcendentals=0),
    )(timestep, attended, modulation, *others)


def per_device(queries, keys, values, queue_state, fresh_state, timestep, window_start, modulation):
    tok_dev, feat = queries.shape
    sections = lax.axis_size("section")
    frame_tok = tok_dev * lax.axis_size("seq") // FRAMES
    packed = pack(queries, keys, values)
    qkv = lax.all_to_all(packed, "seq", split_axis=0, concat_axis=0, tiled=True)
    qkv = qkv.reshape(FRAMES * frame_tok, 3 * HEAD_DIM)
    odd = lax.rem(lax.axis_index("section"), 2)
    facing = [lax.dynamic_slice(qkv, (f * frame_tok, HEAD_DIM), (frame_tok, 2 * HEAD_DIM)) for f in (odd, 1 - odd)]
    pairs = [(i, i + 1) for i in range(1, sections - 1, 2)]
    far = lax.ppermute(facing[0], "section", pairs + [(j, i) for i, j in pairs])
    pairs = [(i, i + 1) for i in range(0, sections - 1, 2)]
    near = lax.ppermute(facing[1], "section", pairs + [(j, i) for i, j in pairs])
    sums, peak = own_part(qkv)
    attended = other_part(window_start, qkv, far, near, sums, peak, sections - 1)
    attended = attended.reshape(feat // HEAD_DIM, tok_dev, HEAD_DIM)
    attended = lax.all_to_all(attended, "seq", split_axis=0, concat_axis=0, tiled=True)
    update = functools.partial(update_kernel, sections - 1)
    passed = finish(update, timestep, attended, modulation, queue_state, fresh_state)
    advanced = lax.ppermute(passed, "section", [(i, (i + 1) % sections) for i in range(sections)])
    velocity = finish(velocity_kernel, timestep, attended, modulation)
    return velocity, advanced


def solution(mesh):
    return jax.shard_map(
        per_device,
        mesh=mesh,
        in_specs=(
            P(("section", "seq"), None),
            P(("section", "seq"), None),
            P(("section", "seq"), None),
            P(("section", "seq"), None),
            P("seq", None),
            P("section"),
            P("section", None),
            P(),
        ),
        out_specs=(P(("section", "seq"), None), P(("section", "seq"), None)),
        check_vma=False,
    )
```

```python
import functools

import jax
import jax.numpy as jnp
from jax import lax
from jax.experimental import pallas as pl
from jax.experimental.pallas import tpu as pltpu
from jax.sharding import PartitionSpec as P

HEAD_DIM = 128
FRAMES = 2
NSTEPS = 16
SCALE = 1.4426950408889634 / HEAD_DIM**0.5
BLOCK = 256
CHUNKS = 2
MORE = 16
VMEM = pl.BlockSpec(memory_space=pltpu.VMEM)
HBM = pl.BlockSpec(memory_space=pltpu.HBM)
SMEM = pl.BlockSpec(memory_space=pltpu.SMEM)
LIMIT = 24 * 1024 * 1024
WHOLE = 63 * 1024 * 1024


def level(step):
    share = step / NSTEPS
    return 5.0 * share / (1.0 + 4.0 * share)


def pack_kernel(q_ref, k_ref, v_ref, out_ref, held_ref, packed_ref, in_sem, out_sem):
    heads = out_ref.shape[0]
    group = heads // CHUNKS
    copies = []
    for chunk in range(CHUNKS):
        cols = slice(chunk * group * HEAD_DIM, (chunk + 1) * group * HEAD_DIM)
        for part, ref in enumerate((q_ref, k_ref, v_ref)):
            copy = pltpu.make_async_copy(ref.at[:, cols], held_ref.at[part, :, cols], in_sem.at[chunk, part])
            copy.start()
            copies.append(copy)
    for chunk in range(CHUNKS):
        mine = slice(chunk * group, (chunk + 1) * group)
        for part in range(3):
            copies[3 * chunk + part].wait()
            for head in range(chunk * group, (chunk + 1) * group):
                cols = slice(head * HEAD_DIM, (head + 1) * HEAD_DIM)
                packed_ref[head, :, part * HEAD_DIM : (part + 1) * HEAD_DIM] = held_ref[part, :, cols]
        copy = pltpu.make_async_copy(packed_ref.at[mine], out_ref.at[mine], out_sem.at[chunk])
        copy.start()
        copies.append(copy)
    for copy in copies[3 * CHUNKS :]:
        copy.wait()


def pack(queries, keys, values):
    tok, feat = queries.shape
    heads = feat // HEAD_DIM
    shape = (heads, tok, 3 * HEAD_DIM)
    return pl.pallas_call(
        pack_kernel,
        in_specs=[HBM] * 3,
        out_specs=HBM,
        out_shape=jax.ShapeDtypeStruct(shape, queries.dtype),
        scratch_shapes=[
            pltpu.VMEM((3, tok, feat), queries.dtype),
            pltpu.VMEM(shape, queries.dtype),
            pltpu.SemaphoreType.DMA((CHUNKS, 3)),
            pltpu.SemaphoreType.DMA((CHUNKS,)),
        ],
        compiler_params=pltpu.CompilerParams(vmem_limit_bytes=WHOLE),
    )(queries, keys, values)


def scores_of(q, keys):
    return lax.dot_general(q, keys, (((1,), (1,)), ((), ())), preferred_element_type=jnp.float32)


def frame_of(far):
    odd = lax.rem(lax.axis_index("section"), 2)
    return odd if far else 1 - odd


def own_kernel(far, qkv_ref, sums_ref, peak_ref, *refs):
    value_ref = refs[-1]
    frame_tok = peak_ref.shape[0]
    first = pl.multiple_of(frame_of(far) * frame_tok, frame_tok)
    own = pl.ds(first, frame_tok)
    if not far:
        refs[0][...] = qkv_ref[own, HEAD_DIM:]
    value_ref[:, :HEAD_DIM] = qkv_ref[own, 2 * HEAD_DIM :]
    value_ref[:, HEAD_DIM:] = jnp.ones((frame_tok, HEAD_DIM), jnp.bfloat16)
    for index in range(frame_tok // BLOCK):
        rows = pl.ds(index * BLOCK, BLOCK)
        q = qkv_ref[pl.ds(pl.multiple_of(first + index * BLOCK, BLOCK), BLOCK), :HEAD_DIM]
        scores = scores_of(q, qkv_ref[own, HEAD_DIM : 2 * HEAD_DIM])
        peak = jnp.max(scores, axis=-1, keepdims=True)
        weights = jnp.exp2((scores - peak) * SCALE).astype(jnp.bfloat16)
        sums_ref[rows, :] = jnp.dot(weights, value_ref[...], preferred_element_type=jnp.float32)
        peak_ref[rows, :] = jnp.broadcast_to(peak, (BLOCK, HEAD_DIM))


def part_cost(frame_tok):
    return pl.CostEstimate(flops=frame_tok, bytes_accessed=frame_tok, transcendentals=0)


def own_part(far, qkv):
    frame_tok = qkv.shape[0] // FRAMES
    shapes = [
        jax.ShapeDtypeStruct((frame_tok, 2 * HEAD_DIM), jnp.float32),
        jax.ShapeDtypeStruct((frame_tok, HEAD_DIM), jnp.float32),
    ]
    if not far:
        shapes.append(jax.ShapeDtypeStruct((frame_tok, 2 * HEAD_DIM), qkv.dtype))
    return pl.pallas_call(
        functools.partial(own_kernel, far),
        in_specs=[VMEM],
        out_specs=[VMEM] * len(shapes),
        out_shape=shapes,
        scratch_shapes=[pltpu.VMEM((frame_tok, 2 * HEAD_DIM), jnp.bfloat16)],
        compiler_params=pltpu.CompilerParams(vmem_limit_bytes=LIMIT),
        cost_estimate=part_cost(frame_tok),
    )(qkv)


def other_frame(final, far, ws_ref, qkv_ref, halo_ref, sums_ref, peak_ref, key_ref, value_ref, store):
    frame_tok = qkv_ref.shape[0] // FRAMES
    position = lax.axis_index("section")
    frame = frame_of(far)
    outside = ws_ref[0, frame] == frame - 1
    exists = jnp.where(frame == 0, position > 0, position < final)
    own = pl.multiple_of(frame * frame_tok, frame_tok)
    other = pl.ds(pl.multiple_of((1 - frame) * frame_tok, frame_tok), frame_tok)
    k_cols, v_cols = slice(HEAD_DIM, 2 * HEAD_DIM), slice(2 * HEAD_DIM, 3 * HEAD_DIM)
    value_ref[:, HEAD_DIM:] = jnp.ones((frame_tok, HEAD_DIM), jnp.bfloat16)

    @pl.when(jnp.logical_not(outside))
    def _():
        key_ref[...] = qkv_ref[other, k_cols]
        value_ref[:, :HEAD_DIM] = qkv_ref[other, v_cols]

    @pl.when(jnp.logical_and(outside, exists))
    def _():
        rows = pl.ds(pl.multiple_of((1 - frame) * MORE, MORE), frame_tok) if far else slice(None)
        key_ref[...] = halo_ref[rows, :HEAD_DIM]
        value_ref[:, :HEAD_DIM] = halo_ref[rows, HEAD_DIM:]

    @pl.when(jnp.logical_and(outside, jnp.logical_not(exists)))
    def _():
        key_ref[...] = qkv_ref[pl.ds(own, frame_tok), k_cols]
        value_ref[...] = jnp.zeros((frame_tok, 2 * HEAD_DIM), jnp.bfloat16)

    def scores(index):
        rows = pl.ds(pl.multiple_of(own + index * BLOCK, BLOCK), BLOCK)
        return scores_of(qkv_ref[rows, :HEAD_DIM], key_ref[...])

    blocks = frame_tok // BLOCK
    after = scores(0)
    for index in range(blocks):
        here = after
        if index + 1 < blocks:
            after = scores(index + 1)
        rows = pl.ds(index * BLOCK, BLOCK)
        before = peak_ref[rows, :]
        peak = jnp.maximum(jnp.broadcast_to(jnp.max(here, axis=-1, keepdims=True), before.shape), before)
        spread = jnp.concatenate([peak] * (frame_tok // HEAD_DIM), axis=1)
        weights = jnp.exp2((here - spread) * SCALE).astype(jnp.bfloat16)
        sums = jnp.dot(weights, value_ref[...], preferred_element_type=jnp.float32)
        share = jnp.exp2((before - peak) * SCALE)
        mixed = sums[:, :HEAD_DIM] + sums_ref[rows, :HEAD_DIM] * share
        total = sums[:, HEAD_DIM:] + sums_ref[rows, HEAD_DIM:] * share
        store(index * BLOCK, (mixed / total).astype(jnp.bfloat16))


def near_kernel(final, ws_ref, qkv_ref, halo_ref, sums_ref, peak_ref, out_ref, key_ref, value_ref):
    def store(begin, result):
        out_ref[pl.ds(begin, BLOCK), :] = result

    other_frame(final, False, ws_ref, qkv_ref, halo_ref, sums_ref, peak_ref, key_ref, value_ref, store)


def far_kernel(final, ws_ref, qkv_ref, halo_ref, sums_ref, peak_ref, near_ref, out_ref, key_ref, value_ref):
    frame_tok = near_ref.shape[0]
    first = frame_of(True) * frame_tok

    def store(begin, result):
        out_ref[pl.ds(pl.multiple_of(first + begin, BLOCK), BLOCK), :] = result

    out_ref[pl.ds(pl.multiple_of(frame_of(False) * frame_tok, frame_tok), frame_tok), :] = near_ref[...]
    other_frame(final, True, ws_ref, qkv_ref, halo_ref, sums_ref, peak_ref, key_ref, value_ref, store)


def other_part(kernel, rows, window_start, qkv, *others):
    frame_tok = qkv.shape[0] // FRAMES
    return pl.pallas_call(
        kernel,
        in_specs=[SMEM] + [VMEM] * (1 + len(others)),
        out_specs=VMEM,
        out_shape=jax.ShapeDtypeStruct((rows, HEAD_DIM), qkv.dtype),
        scratch_shapes=[
            pltpu.VMEM((frame_tok, HEAD_DIM), jnp.bfloat16),
            pltpu.VMEM((frame_tok, 2 * HEAD_DIM), jnp.bfloat16),
        ],
        compiler_params=pltpu.CompilerParams(vmem_limit_bytes=LIMIT),
        cost_estimate=part_cost(frame_tok),
    )(window_start, qkv, *others)


def velocity_of(step_ref, att_ref, mod_ref):
    heads, tok, _ = att_ref.shape
    squares = jnp.zeros((tok, HEAD_DIM), jnp.float32)
    for head in range(heads):
        a = att_ref[head].astype(jnp.float32)
        squares += a * a
    mean = jnp.sum(squares, axis=-1, keepdims=True) / (heads * HEAD_DIM)
    inverse = jnp.broadcast_to(1.0 / jnp.sqrt(mean + 1e-06), (tok, HEAD_DIM))
    chosen = lax.broadcasted_iota(jnp.int32, (NSTEPS, HEAD_DIM), 0) == step_ref[0]
    for head in range(heads):
        cols = slice(head * HEAD_DIM, (head + 1) * HEAD_DIM)
        gain = jnp.sum(jnp.where(chosen, mod_ref[:, cols], 0.0), axis=0, keepdims=True)
        yield cols, att_ref[head].astype(jnp.float32) * inverse * gain


def update_kernel(final, step_ref, att_ref, mod_ref, state_ref, fresh_ref, passed_ref):
    now = jnp.full((1, HEAD_DIM), step_ref[0], jnp.int32)
    delta = level((now - 1).astype(jnp.float32)) - level(now.astype(jnp.float32))
    for cols, moving in velocity_of(step_ref, att_ref, mod_ref):
        passed_ref[:, cols] = (state_ref[:, cols].astype(jnp.float32) + delta * moving).astype(jnp.bfloat16)

    @pl.when(lax.axis_index("section") == final)
    def _():
        passed_ref[...] = fresh_ref[...]


def velocity_kernel(step_ref, att_ref, mod_ref, velocity_ref):
    for cols, moving in velocity_of(step_ref, att_ref, mod_ref):
        velocity_ref[:, cols] = moving.astype(jnp.bfloat16)


def finish(kernel, timestep, attended, modulation, *others):
    heads, tok, _ = attended.shape
    return pl.pallas_call(
        kernel,
        in_specs=[SMEM] + [VMEM] * (2 + len(others)),
        out_specs=VMEM,
        out_shape=jax.ShapeDtypeStruct((tok, heads * HEAD_DIM), attended.dtype),
        compiler_params=pltpu.CompilerParams(vmem_limit_bytes=LIMIT),
        cost_estimate=pl.CostEstimate(flops=10 * tok * heads * HEAD_DIM, bytes_accessed=6 * tok * heads * HEAD_DIM, transcendentals=0),
    )(timestep, attended, modulation, *others)


def per_device(queries, keys, values, queue_state, fresh_state, timestep, window_start, modulation):
    tok_dev, feat = queries.shape
    sections = lax.axis_size("section")
    frame_tok = tok_dev * lax.axis_size("seq") // FRAMES
    packed = pack(queries, keys, values)
    qkv = lax.all_to_all(packed, "seq", split_axis=0, concat_axis=0, tiled=True)
    qkv = qkv.reshape(FRAMES * frame_tok, 3 * HEAD_DIM)
    start = frame_of(True) * (frame_tok - MORE)
    facing = lax.dynamic_slice(qkv, (start, HEAD_DIM), (frame_tok + MORE, 2 * HEAD_DIM))
    pairs = [(i, i + 1) for i in range(1, sections - 1, 2)]
    far = lax.ppermute(facing, "section", pairs + [(j, i) for i, j in pairs])
    near_sums, near_peak, facing = own_part(False, qkv)
    pairs = [(i, i + 1) for i in range(0, sections - 1, 2)]
    near = lax.ppermute(facing, "section", pairs + [(j, i) for i, j in pairs])
    far_sums, far_peak = own_part(True, qkv)
    kernels = [functools.partial(kernel, sections - 1) for kernel in (near_kernel, far_kernel)]
    near_out = other_part(kernels[0], frame_tok, window_start, qkv, near, near_sums, near_peak)
    attended = other_part(kernels[1], FRAMES * frame_tok, window_start, qkv, far, far_sums, far_peak, near_out)
    attended = attended.reshape(feat // HEAD_DIM, tok_dev, HEAD_DIM)
    attended = lax.all_to_all(attended, "seq", split_axis=0, concat_axis=0, tiled=True)
    update = functools.partial(update_kernel, sections - 1)
    passed = finish(update, timestep, attended, modulation, queue_state, fresh_state)
    advanced = lax.ppermute(passed, "section", [(i, (i + 1) % sections) for i in range(sections)])
    velocity = finish(velocity_kernel, timestep, attended, modulation)
    return velocity, advanced


def solution(mesh):
    return jax.shard_map(
        per_device,
        mesh=mesh,
        in_specs=(
            P(("section", "seq"), None),
            P(("section", "seq"), None),
            P(("section", "seq"), None),
            P(("section", "seq"), None),
            P("seq", None),
            P("section"),
            P("section", None),
            P(),
        ),
        out_specs=(P(("section", "seq"), None), P(("section", "seq"), None)),
        check_vma=False,
    )
```

```python
import functools

import jax
import jax.numpy as jnp
from jax import lax
from jax.experimental import pallas as pl
from jax.experimental.pallas import tpu as pltpu
from jax.sharding import PartitionSpec as P

HEAD_DIM = 128
FRAMES = 2
NSTEPS = 16
SCALE = 1.4426950408889634 / HEAD_DIM**0.5
BLOCK = 256
CHUNKS = 2
MORE = 16
VMEM = pl.BlockSpec(memory_space=pltpu.VMEM)
HBM = pl.BlockSpec(memory_space=pltpu.HBM)
SMEM = pl.BlockSpec(memory_space=pltpu.SMEM)
LIMIT = 24 * 1024 * 1024
WHOLE = 63 * 1024 * 1024


def level(step):
    share = step / NSTEPS
    return 5.0 * share / (1.0 + 4.0 * share)


def pack_kernel(q_ref, k_ref, v_ref, out_ref, held_ref, packed_ref, in_sem, out_sem):
    heads = out_ref.shape[0]
    group = heads // CHUNKS
    copies = []
    for chunk in range(CHUNKS):
        cols = slice(chunk * group * HEAD_DIM, (chunk + 1) * group * HEAD_DIM)
        for part, ref in enumerate((q_ref, k_ref, v_ref)):
            copy = pltpu.make_async_copy(ref.at[:, cols], held_ref.at[part, :, cols], in_sem.at[chunk, part])
            copy.start()
            copies.append(copy)
    for chunk in range(CHUNKS):
        mine = slice(chunk * group, (chunk + 1) * group)
        for part in range(3):
            copies[3 * chunk + part].wait()
            for head in range(chunk * group, (chunk + 1) * group):
                cols = slice(head * HEAD_DIM, (head + 1) * HEAD_DIM)
                packed_ref[head, :, part * HEAD_DIM : (part + 1) * HEAD_DIM] = held_ref[part, :, cols]
        copy = pltpu.make_async_copy(packed_ref.at[mine], out_ref.at[mine], out_sem.at[chunk])
        copy.start()
        copies.append(copy)
    for copy in copies[3 * CHUNKS :]:
        copy.wait()


def pack(queries, keys, values):
    tok, feat = queries.shape
    heads = feat // HEAD_DIM
    shape = (heads, tok, 3 * HEAD_DIM)
    return pl.pallas_call(
        pack_kernel,
        in_specs=[HBM] * 3,
        out_specs=HBM,
        out_shape=jax.ShapeDtypeStruct(shape, queries.dtype),
        scratch_shapes=[
            pltpu.VMEM((3, tok, feat), queries.dtype),
            pltpu.VMEM(shape, queries.dtype),
            pltpu.SemaphoreType.DMA((CHUNKS, 3)),
            pltpu.SemaphoreType.DMA((CHUNKS,)),
        ],
        compiler_params=pltpu.CompilerParams(vmem_limit_bytes=WHOLE),
    )(queries, keys, values)


def scores_of(q, keys):
    return lax.dot_general(q, keys, (((1,), (1,)), ((), ())), preferred_element_type=jnp.float32)


def frame_of(far):
    odd = lax.rem(lax.axis_index("section"), 2)
    return odd if far else 1 - odd


def own_kernel(far, qkv_ref, sums_ref, peak_ref, value_ref):
    frame_tok = peak_ref.shape[0]
    first = pl.multiple_of(frame_of(far) * frame_tok, frame_tok)
    own = pl.ds(first, frame_tok)
    value_ref[:, :HEAD_DIM] = qkv_ref[own, 2 * HEAD_DIM :]
    value_ref[:, HEAD_DIM:] = jnp.ones((frame_tok, HEAD_DIM), jnp.bfloat16)
    for index in range(frame_tok // BLOCK):
        rows = pl.ds(index * BLOCK, BLOCK)
        q = qkv_ref[pl.ds(pl.multiple_of(first + index * BLOCK, BLOCK), BLOCK), :HEAD_DIM]
        scores = scores_of(q, qkv_ref[own, HEAD_DIM : 2 * HEAD_DIM])
        peak = jnp.max(scores, axis=-1, keepdims=True)
        weights = jnp.exp2((scores - peak) * SCALE).astype(jnp.bfloat16)
        sums_ref[rows, :] = jnp.dot(weights, value_ref[...], preferred_element_type=jnp.float32)
        peak_ref[rows, :] = jnp.broadcast_to(peak, (BLOCK, HEAD_DIM))


def part_cost(frame_tok):
    return pl.CostEstimate(flops=frame_tok, bytes_accessed=frame_tok, transcendentals=0)


def own_part(far, qkv):
    frame_tok = qkv.shape[0] // FRAMES
    shapes = [
        jax.ShapeDtypeStruct((frame_tok, 2 * HEAD_DIM), jnp.float32),
        jax.ShapeDtypeStruct((frame_tok, HEAD_DIM), jnp.float32),
    ]
    return pl.pallas_call(
        functools.partial(own_kernel, far),
        in_specs=[VMEM],
        out_specs=[VMEM] * len(shapes),
        out_shape=shapes,
        scratch_shapes=[pltpu.VMEM((frame_tok, 2 * HEAD_DIM), jnp.bfloat16)],
        compiler_params=pltpu.CompilerParams(vmem_limit_bytes=LIMIT),
        cost_estimate=part_cost(frame_tok),
    )(qkv)


def other_frame(final, far, ws_ref, qkv_ref, halo_ref, sums_ref, peak_ref, key_ref, value_ref, store):
    frame_tok = qkv_ref.shape[0] // FRAMES
    position = lax.axis_index("section")
    frame = frame_of(far)
    outside = ws_ref[0, frame] == frame - 1
    exists = jnp.where(frame == 0, position > 0, position < final)
    own = pl.multiple_of(frame * frame_tok, frame_tok)
    other = pl.ds(pl.multiple_of((1 - frame) * frame_tok, frame_tok), frame_tok)
    k_cols, v_cols = slice(HEAD_DIM, 2 * HEAD_DIM), slice(2 * HEAD_DIM, 3 * HEAD_DIM)
    value_ref[:, HEAD_DIM:] = jnp.ones((frame_tok, HEAD_DIM), jnp.bfloat16)

    @pl.when(jnp.logical_not(outside))
    def _():
        key_ref[...] = qkv_ref[other, k_cols]
        value_ref[:, :HEAD_DIM] = qkv_ref[other, v_cols]

    @pl.when(jnp.logical_and(outside, exists))
    def _():
        rows = pl.ds(pl.multiple_of((1 - frame) * MORE, MORE), frame_tok) if far else slice(None)
        key_ref[...] = halo_ref[rows, :HEAD_DIM]
        value_ref[:, :HEAD_DIM] = halo_ref[rows, HEAD_DIM:]

    @pl.when(jnp.logical_and(outside, jnp.logical_not(exists)))
    def _():
        key_ref[...] = qkv_ref[pl.ds(own, frame_tok), k_cols]
        value_ref[...] = jnp.zeros((frame_tok, 2 * HEAD_DIM), jnp.bfloat16)

    def scores(index):
        rows = pl.ds(pl.multiple_of(own + index * BLOCK, BLOCK), BLOCK)
        return scores_of(qkv_ref[rows, :HEAD_DIM], key_ref[...])

    blocks = frame_tok // BLOCK
    after = scores(0)
    for index in range(blocks):
        here = after
        if index + 1 < blocks:
            after = scores(index + 1)
        rows = pl.ds(index * BLOCK, BLOCK)
        before = peak_ref[rows, :]
        peak = jnp.maximum(jnp.broadcast_to(jnp.max(here, axis=-1, keepdims=True), before.shape), before)
        spread = jnp.concatenate([peak] * (frame_tok // HEAD_DIM), axis=1)
        weights = jnp.exp2((here - spread) * SCALE).astype(jnp.bfloat16)
        sums = jnp.dot(weights, value_ref[...], preferred_element_type=jnp.float32)
        share = jnp.exp2((before - peak) * SCALE)
        mixed = sums[:, :HEAD_DIM] + sums_ref[rows, :HEAD_DIM] * share
        total = sums[:, HEAD_DIM:] + sums_ref[rows, HEAD_DIM:] * share
        store(index * BLOCK, (mixed / total).astype(jnp.bfloat16))


def near_kernel(final, ws_ref, qkv_ref, halo_ref, sums_ref, peak_ref, out_ref, key_ref, value_ref):
    def store(begin, result):
        out_ref[pl.ds(begin, BLOCK), :] = result

    other_frame(final, False, ws_ref, qkv_ref, halo_ref, sums_ref, peak_ref, key_ref, value_ref, store)


def far_kernel(final, ws_ref, qkv_ref, halo_ref, sums_ref, peak_ref, near_ref, out_ref, key_ref, value_ref, held_ref, sem_ref):
    frame_tok = near_ref.shape[0]
    first = frame_of(True) * frame_tok
    rest = pl.ds(pl.multiple_of(frame_of(False) * frame_tok, frame_tok), frame_tok)
    copies = [pltpu.make_async_copy(near_ref, out_ref.at[rest], sem_ref.at[0])]
    copies[0].start()

    def store(begin, result):
        rows = pl.ds(begin, BLOCK)
        held_ref[rows, :] = result
        there = out_ref.at[pl.ds(pl.multiple_of(first + begin, BLOCK), BLOCK)]
        copies.append(pltpu.make_async_copy(held_ref.at[rows], there, sem_ref.at[len(copies)]))
        copies[-1].start()

    other_frame(final, True, ws_ref, qkv_ref, halo_ref, sums_ref, peak_ref, key_ref, value_ref, store)
    for copy in copies:
        copy.wait()


def other_part(far, final, window_start, qkv, *others):
    frame_tok = qkv.shape[0] // FRAMES
    out = jax.ShapeDtypeStruct((FRAMES * frame_tok if far else frame_tok, HEAD_DIM), qkv.dtype)
    scratch = [pltpu.VMEM((frame_tok, HEAD_DIM), jnp.bfloat16), pltpu.VMEM((frame_tok, 2 * HEAD_DIM), jnp.bfloat16)]
    if far:
        scratch += [pltpu.VMEM((frame_tok, HEAD_DIM), jnp.bfloat16), pltpu.SemaphoreType.DMA((1 + frame_tok // BLOCK,))]
    return pl.pallas_call(
        functools.partial(far_kernel if far else near_kernel, final),
        in_specs=[SMEM] + [VMEM] * (1 + len(others)),
        out_specs=HBM if far else VMEM,
        out_shape=out,
        scratch_shapes=scratch,
        compiler_params=pltpu.CompilerParams(vmem_limit_bytes=LIMIT),
        cost_estimate=part_cost(frame_tok),
    )(window_start, qkv, *others)


def velocity_of(step_ref, att_ref, mod_ref):
    heads, tok, _ = att_ref.shape
    squares = jnp.zeros((tok, HEAD_DIM), jnp.float32)
    for head in range(heads):
        a = att_ref[head].astype(jnp.float32)
        squares += a * a
    mean = jnp.sum(squares, axis=-1, keepdims=True) / (heads * HEAD_DIM)
    inverse = jnp.broadcast_to(1.0 / jnp.sqrt(mean + 1e-06), (tok, HEAD_DIM))
    chosen = lax.broadcasted_iota(jnp.int32, (NSTEPS, HEAD_DIM), 0) == step_ref[0]
    for head in range(heads):
        cols = slice(head * HEAD_DIM, (head + 1) * HEAD_DIM)
        gain = jnp.sum(jnp.where(chosen, mod_ref[:, cols], 0.0), axis=0, keepdims=True)
        yield cols, att_ref[head].astype(jnp.float32) * inverse * gain


def update_kernel(final, step_ref, att_ref, mod_ref, state_ref, fresh_ref, passed_ref):
    now = jnp.full((1, HEAD_DIM), step_ref[0], jnp.int32)
    delta = level((now - 1).astype(jnp.float32)) - level(now.astype(jnp.float32))
    for cols, moving in velocity_of(step_ref, att_ref, mod_ref):
        passed_ref[:, cols] = (state_ref[:, cols].astype(jnp.float32) + delta * moving).astype(jnp.bfloat16)

    @pl.when(lax.axis_index("section") == final)
    def _():
        passed_ref[...] = fresh_ref[...]


def velocity_kernel(step_ref, att_ref, mod_ref, velocity_ref):
    for cols, moving in velocity_of(step_ref, att_ref, mod_ref):
        velocity_ref[:, cols] = moving.astype(jnp.bfloat16)


def finish(kernel, timestep, attended, modulation, *others):
    heads, tok, _ = attended.shape
    return pl.pallas_call(
        kernel,
        in_specs=[SMEM] + [VMEM] * (2 + len(others)),
        out_specs=VMEM,
        out_shape=jax.ShapeDtypeStruct((tok, heads * HEAD_DIM), attended.dtype),
        compiler_params=pltpu.CompilerParams(vmem_limit_bytes=LIMIT),
        cost_estimate=pl.CostEstimate(flops=10 * tok * heads * HEAD_DIM, bytes_accessed=6 * tok * heads * HEAD_DIM, transcendentals=0),
    )(timestep, attended, modulation, *others)


def per_device(queries, keys, values, queue_state, fresh_state, timestep, window_start, modulation):
    tok_dev, feat = queries.shape
    sections = lax.axis_size("section")
    frame_tok = tok_dev * lax.axis_size("seq") // FRAMES
    packed = pack(queries, keys, values)
    qkv = lax.all_to_all(packed, "seq", split_axis=0, concat_axis=0, tiled=True)
    qkv = qkv.reshape(FRAMES * frame_tok, 3 * HEAD_DIM)
    start = frame_of(True) * (frame_tok - MORE)
    facing = lax.dynamic_slice(qkv, (start, HEAD_DIM), (frame_tok + MORE, 2 * HEAD_DIM))
    pairs = [(i, i + 1) for i in range(1, sections - 1, 2)]
    far = lax.ppermute(facing, "section", pairs + [(j, i) for i, j in pairs])
    facing = lax.dynamic_slice(qkv, (frame_of(False) * frame_tok, HEAD_DIM), (frame_tok, 2 * HEAD_DIM))
    pairs = [(i, i + 1) for i in range(0, sections - 1, 2)]
    near = lax.ppermute(facing, "section", pairs + [(j, i) for i, j in pairs])
    near_sums, near_peak = own_part(False, qkv)
    far_sums, far_peak = own_part(True, qkv)
    near_out = other_part(False, sections - 1, window_start, qkv, near, near_sums, near_peak)
    attended = other_part(True, sections - 1, window_start, qkv, far, far_sums, far_peak, near_out)
    attended = attended.reshape(feat // HEAD_DIM, tok_dev, HEAD_DIM)
    attended = lax.all_to_all(attended, "seq", split_axis=0, concat_axis=0, tiled=True)
    update = functools.partial(update_kernel, sections - 1)
    passed = finish(update, timestep, attended, modulation, queue_state, fresh_state)
    advanced = lax.ppermute(passed, "section", [(i, (i + 1) % sections) for i in range(sections)])
    velocity = finish(velocity_kernel, timestep, attended, modulation)
    return velocity, advanced


def solution(mesh):
    return jax.shard_map(
        per_device,
        mesh=mesh,
        in_specs=(
            P(("section", "seq"), None),
            P(("section", "seq"), None),
            P(("section", "seq"), None),
            P(("section", "seq"), None),
            P("seq", None),
            P("section"),
            P("section", None),
            P(),
        ),
        out_specs=(P(("section", "seq"), None), P(("section", "seq"), None)),
        check_vma=False,
    )
```

```python
import functools

import jax
import jax.numpy as jnp
from jax import lax
from jax.experimental import pallas as pl
from jax.experimental.pallas import tpu as pltpu
from jax.sharding import PartitionSpec as P

HEAD_DIM = 128
FRAMES = 2
NSTEPS = 16
SCALE = 1.4426950408889634 / HEAD_DIM**0.5
BLOCK = 256
CHUNKS = 4
MORE = 16
VMEM = pl.BlockSpec(memory_space=pltpu.VMEM)
HBM = pl.BlockSpec(memory_space=pltpu.HBM)
SMEM = pl.BlockSpec(memory_space=pltpu.SMEM)
LIMIT = 24 * 1024 * 1024
WHOLE = 63 * 1024 * 1024


def level(step):
    share = step / NSTEPS
    return 5.0 * share / (1.0 + 4.0 * share)


def pack_kernel(q_ref, k_ref, v_ref, out_ref, packed_ref, in_sem, out_sem):
    heads = out_ref.shape[0]
    group = heads // CHUNKS
    for head in range(heads):
        cols = slice(head * HEAD_DIM, (head + 1) * HEAD_DIM)
        for part, ref in enumerate((q_ref, k_ref, v_ref)):
            there = packed_ref.at[head, :, part * HEAD_DIM : (part + 1) * HEAD_DIM]
            pltpu.make_async_copy(ref.at[:, cols], there, in_sem.at[head // group]).start()
    leaving = []
    for chunk in range(CHUNKS):
        mine = packed_ref.at[chunk * group : (chunk + 1) * group]
        pltpu.make_async_copy(mine, mine, in_sem.at[chunk]).wait()
        there = out_ref.at[chunk * group : (chunk + 1) * group]
        leaving.append(pltpu.make_async_copy(mine, there, out_sem.at[chunk]))
        leaving[-1].start()
    for copy in leaving:
        copy.wait()


def pack(queries, keys, values):
    tok, feat = queries.shape
    heads = feat // HEAD_DIM
    shape = (heads, tok, 3 * HEAD_DIM)
    return pl.pallas_call(
        pack_kernel,
        in_specs=[HBM] * 3,
        out_specs=HBM,
        out_shape=jax.ShapeDtypeStruct(shape, queries.dtype),
        scratch_shapes=[
            pltpu.VMEM(shape, queries.dtype),
            pltpu.SemaphoreType.DMA((CHUNKS,)),
            pltpu.SemaphoreType.DMA((CHUNKS,)),
        ],
        compiler_params=pltpu.CompilerParams(vmem_limit_bytes=WHOLE),
    )(queries, keys, values)


def scores_of(q, keys):
    return lax.dot_general(q, keys, (((1,), (1,)), ((), ())), preferred_element_type=jnp.float32)


def frame_of(far):
    odd = lax.rem(lax.axis_index("section"), 2)
    return odd if far else 1 - odd


def own_kernel(qkv_ref, sums_ref, peak_ref, value_ref):
    frame_tok = peak_ref.shape[0]
    first = pl.multiple_of(frame_of(True) * frame_tok, frame_tok)
    own = pl.ds(first, frame_tok)
    value_ref[:, :HEAD_DIM] = qkv_ref[own, 2 * HEAD_DIM :]
    value_ref[:, HEAD_DIM:] = jnp.ones((frame_tok, HEAD_DIM), jnp.bfloat16)
    for index in range(frame_tok // BLOCK):
        rows = pl.ds(index * BLOCK, BLOCK)
        q = qkv_ref[pl.ds(pl.multiple_of(first + index * BLOCK, BLOCK), BLOCK), :HEAD_DIM]
        scores = scores_of(q, qkv_ref[own, HEAD_DIM : 2 * HEAD_DIM])
        peak = jnp.max(scores, axis=-1, keepdims=True)
        weights = jnp.exp2((scores - peak) * SCALE).astype(jnp.bfloat16)
        sums_ref[rows, :] = jnp.dot(weights, value_ref[...], preferred_element_type=jnp.float32)
        peak_ref[rows, :] = jnp.broadcast_to(peak, (BLOCK, HEAD_DIM))


def part_cost(frame_tok):
    return pl.CostEstimate(flops=frame_tok, bytes_accessed=frame_tok, transcendentals=0)


def own_part(qkv):
    frame_tok = qkv.shape[0] // FRAMES
    shapes = [
        jax.ShapeDtypeStruct((frame_tok, 2 * HEAD_DIM), jnp.float32),
        jax.ShapeDtypeStruct((frame_tok, HEAD_DIM), jnp.float32),
    ]
    return pl.pallas_call(
        own_kernel,
        in_specs=[VMEM],
        out_specs=[VMEM] * len(shapes),
        out_shape=shapes,
        scratch_shapes=[pltpu.VMEM((frame_tok, 2 * HEAD_DIM), jnp.bfloat16)],
        compiler_params=pltpu.CompilerParams(vmem_limit_bytes=LIMIT),
        cost_estimate=part_cost(frame_tok),
    )(qkv)


def other_frame(final, far, ws_ref, qkv_ref, halo_ref, key_ref, value_ref):
    frame_tok = qkv_ref.shape[0] // FRAMES
    position = lax.axis_index("section")
    frame = frame_of(far)
    outside = ws_ref[0, frame] == frame - 1
    exists = jnp.where(frame == 0, position > 0, position < final)
    own = pl.ds(pl.multiple_of(frame * frame_tok, frame_tok), frame_tok)
    other = pl.ds(pl.multiple_of((1 - frame) * frame_tok, frame_tok), frame_tok)
    k_cols, v_cols = slice(HEAD_DIM, 2 * HEAD_DIM), slice(2 * HEAD_DIM, 3 * HEAD_DIM)
    value_ref[:, HEAD_DIM:] = jnp.ones((frame_tok, HEAD_DIM), jnp.bfloat16)

    @pl.when(jnp.logical_not(outside))
    def _():
        key_ref[...] = qkv_ref[other, k_cols]
        value_ref[:, :HEAD_DIM] = qkv_ref[other, v_cols]

    @pl.when(jnp.logical_and(outside, exists))
    def _():
        rows = pl.ds(pl.multiple_of((1 - frame) * MORE, MORE), frame_tok) if far else slice(None)
        key_ref[...] = halo_ref[rows, :HEAD_DIM]
        value_ref[:, :HEAD_DIM] = halo_ref[rows, HEAD_DIM:]

    @pl.when(jnp.logical_and(outside, jnp.logical_not(exists)))
    def _():
        key_ref[...] = qkv_ref[own, k_cols]
        value_ref[...] = jnp.zeros((frame_tok, 2 * HEAD_DIM), jnp.bfloat16)


def near_kernel(final, ws_ref, qkv_ref, halo_ref, out_ref, key_ref, value_ref):
    frame_tok = out_ref.shape[0]
    first = pl.multiple_of(frame_of(False) * frame_tok, frame_tok)
    own, rest = pl.ds(first, frame_tok), pl.ds(frame_tok, frame_tok)
    key_ref[:frame_tok] = qkv_ref[own, HEAD_DIM : 2 * HEAD_DIM]
    value_ref[:frame_tok, :HEAD_DIM] = qkv_ref[own, 2 * HEAD_DIM :]
    value_ref[:frame_tok, HEAD_DIM:] = jnp.ones((frame_tok, HEAD_DIM), jnp.bfloat16)
    other_frame(final, False, ws_ref, qkv_ref, halo_ref, key_ref.at[rest], value_ref.at[rest])

    def scores(index):
        rows = pl.ds(pl.multiple_of(first + index * BLOCK, BLOCK), BLOCK)
        return scores_of(qkv_ref[rows, :HEAD_DIM], key_ref[...])

    blocks = frame_tok // BLOCK
    after = scores(0)
    for index in range(blocks):
        here = after
        if index + 1 < blocks:
            after = scores(index + 1)
        peak = jnp.max(here, axis=-1, keepdims=True)
        weights = jnp.exp2((here - peak) * SCALE).astype(jnp.bfloat16)
        sums = jnp.dot(weights, value_ref[...], preferred_element_type=jnp.float32)
        result = (sums[:, :HEAD_DIM] / sums[:, HEAD_DIM:]).astype(jnp.bfloat16)
        out_ref[index * BLOCK : (index + 1) * BLOCK, :] = result


def far_kernel(final, ws_ref, qkv_ref, halo_ref, sums_ref, peak_ref, near_ref, out_ref, key_ref, value_ref, held_ref, sem_ref):
    frame_tok = near_ref.shape[0]
    first = pl.multiple_of(frame_of(True) * frame_tok, frame_tok)
    rest = pl.ds(pl.multiple_of(frame_of(False) * frame_tok, frame_tok), frame_tok)
    copies = [pltpu.make_async_copy(near_ref, out_ref.at[rest], sem_ref.at[0])]
    copies[0].start()
    other_frame(final, True, ws_ref, qkv_ref, halo_ref, key_ref, value_ref)

    def scores(index):
        rows = pl.ds(pl.multiple_of(first + index * BLOCK, BLOCK), BLOCK)
        return scores_of(qkv_ref[rows, :HEAD_DIM], key_ref[...])

    blocks = frame_tok // BLOCK
    after = scores(0)
    for index in range(blocks):
        here = after
        if index + 1 < blocks:
            after = scores(index + 1)
        rows = pl.ds(index * BLOCK, BLOCK)
        before = peak_ref[rows, :]
        peak = jnp.maximum(jnp.broadcast_to(jnp.max(here, axis=-1, keepdims=True), before.shape), before)
        spread = jnp.concatenate([peak] * (frame_tok // HEAD_DIM), axis=1)
        weights = jnp.exp2((here - spread) * SCALE).astype(jnp.bfloat16)
        sums = jnp.dot(weights, value_ref[...], preferred_element_type=jnp.float32)
        share = jnp.exp2((before - peak) * SCALE)
        mixed = sums[:, :HEAD_DIM] + sums_ref[rows, :HEAD_DIM] * share
        total = sums[:, HEAD_DIM:] + sums_ref[rows, HEAD_DIM:] * share
        held_ref[rows, :] = (mixed / total).astype(jnp.bfloat16)
        there = out_ref.at[pl.ds(pl.multiple_of(first + index * BLOCK, BLOCK), BLOCK)]
        copies.append(pltpu.make_async_copy(held_ref.at[rows], there, sem_ref.at[1 + index]))
        copies[-1].start()
    for copy in copies:
        copy.wait()


def window_part(far, final, window_start, qkv, *others):
    frame_tok = qkv.shape[0] // FRAMES
    out = jax.ShapeDtypeStruct((FRAMES * frame_tok if far else frame_tok, HEAD_DIM), qkv.dtype)
    keys = frame_tok if far else FRAMES * frame_tok
    scratch = [pltpu.VMEM((keys, HEAD_DIM), jnp.bfloat16), pltpu.VMEM((keys, 2 * HEAD_DIM), jnp.bfloat16)]
    if far:
        scratch += [pltpu.VMEM((frame_tok, HEAD_DIM), jnp.bfloat16), pltpu.SemaphoreType.DMA((1 + frame_tok // BLOCK,))]
    return pl.pallas_call(
        functools.partial(far_kernel if far else near_kernel, final),
        in_specs=[SMEM] + [VMEM] * (1 + len(others)),
        out_specs=HBM if far else VMEM,
        out_shape=out,
        scratch_shapes=scratch,
        compiler_params=pltpu.CompilerParams(vmem_limit_bytes=LIMIT),
        cost_estimate=part_cost(frame_tok),
    )(window_start, qkv, *others)


def velocity_of(step_ref, att_ref, mod_ref):
    heads, tok, _ = att_ref.shape
    squares = jnp.zeros((tok, HEAD_DIM), jnp.float32)
    for head in range(heads):
        a = att_ref[head].astype(jnp.float32)
        squares += a * a
    mean = jnp.sum(squares, axis=-1, keepdims=True) / (heads * HEAD_DIM)
    inverse = jnp.broadcast_to(1.0 / jnp.sqrt(mean + 1e-06), (tok, HEAD_DIM))
    chosen = lax.broadcasted_iota(jnp.int32, (NSTEPS, HEAD_DIM), 0) == step_ref[0]
    for head in range(heads):
        cols = slice(head * HEAD_DIM, (head + 1) * HEAD_DIM)
        gain = jnp.sum(jnp.where(chosen, mod_ref[:, cols], 0.0), axis=0, keepdims=True)
        yield cols, att_ref[head].astype(jnp.float32) * inverse * gain


def update_kernel(final, step_ref, att_ref, mod_ref, state_ref, fresh_ref, passed_ref):
    now = jnp.full((1, HEAD_DIM), step_ref[0], jnp.int32)
    delta = level((now - 1).astype(jnp.float32)) - level(now.astype(jnp.float32))
    for cols, moving in velocity_of(step_ref, att_ref, mod_ref):
        passed_ref[:, cols] = (state_ref[:, cols].astype(jnp.float32) + delta * moving).astype(jnp.bfloat16)

    @pl.when(lax.axis_index("section") == final)
    def _():
        passed_ref[...] = fresh_ref[...]


def velocity_kernel(step_ref, att_ref, mod_ref, velocity_ref):
    for cols, moving in velocity_of(step_ref, att_ref, mod_ref):
        velocity_ref[:, cols] = moving.astype(jnp.bfloat16)


def finish(kernel, timestep, attended, modulation, *others):
    heads, tok, _ = attended.shape
    return pl.pallas_call(
        kernel,
        in_specs=[SMEM] + [VMEM] * (2 + len(others)),
        out_specs=VMEM,
        out_shape=jax.ShapeDtypeStruct((tok, heads * HEAD_DIM), attended.dtype),
        compiler_params=pltpu.CompilerParams(vmem_limit_bytes=LIMIT),
        cost_estimate=pl.CostEstimate(flops=10 * tok * heads * HEAD_DIM, bytes_accessed=6 * tok * heads * HEAD_DIM, transcendentals=0),
    )(timestep, attended, modulation, *others)


def per_device(queries, keys, values, queue_state, fresh_state, timestep, window_start, modulation):
    tok_dev, feat = queries.shape
    sections = lax.axis_size("section")
    frame_tok = tok_dev * lax.axis_size("seq") // FRAMES
    packed = pack(queries, keys, values)
    qkv = lax.all_to_all(packed, "seq", split_axis=0, concat_axis=0, tiled=True)
    qkv = qkv.reshape(FRAMES * frame_tok, 3 * HEAD_DIM)
    start = frame_of(True) * (frame_tok - MORE)
    facing = lax.dynamic_slice(qkv, (start, HEAD_DIM), (frame_tok + MORE, 2 * HEAD_DIM))
    pairs = [(i, i + 1) for i in range(1, sections - 1, 2)]
    far = lax.ppermute(facing, "section", pairs + [(j, i) for i, j in pairs])
    facing = lax.dynamic_slice(qkv, (frame_of(False) * frame_tok, HEAD_DIM), (frame_tok, 2 * HEAD_DIM))
    pairs = [(i, i + 1) for i in range(0, sections - 1, 2)]
    near = lax.ppermute(facing, "section", pairs + [(j, i) for i, j in pairs])
    sums, peak = own_part(qkv)
    near_out = window_part(False, sections - 1, window_start, qkv, near)
    attended = window_part(True, sections - 1, window_start, qkv, far, sums, peak, near_out)
    attended = attended.reshape(feat // HEAD_DIM, tok_dev, HEAD_DIM)
    attended = lax.all_to_all(attended, "seq", split_axis=0, concat_axis=0, tiled=True)
    update = functools.partial(update_kernel, sections - 1)
    passed = finish(update, timestep, attended, modulation, queue_state, fresh_state)
    advanced = lax.ppermute(passed, "section", [(i, (i + 1) % sections) for i in range(sections)])
    velocity = finish(velocity_kernel, timestep, attended, modulation)
    return velocity, advanced


def solution(mesh):
    return jax.shard_map(
        per_device,
        mesh=mesh,
        in_specs=(
            P(("section", "seq"), None),
            P(("section", "seq"), None),
            P(("section", "seq"), None),
            P(("section", "seq"), None),
            P("seq", None),
            P("section"),
            P("section", None),
            P(),
        ),
        out_specs=(P(("section", "seq"), None), P(("section", "seq"), None)),
        check_vma=False,
    )
```

```python
import functools

import jax
import jax.numpy as jnp
from jax import lax
from jax.experimental import pallas as pl
from jax.experimental.pallas import tpu as pltpu
from jax.sharding import PartitionSpec as P

HEAD_DIM = 128
FRAMES = 2
NSTEPS = 16
SCALE = 1.4426950408889634 / HEAD_DIM**0.5
BLOCK = 256
CHUNKS = 4
MORE = 16
VMEM = pl.BlockSpec(memory_space=pltpu.VMEM)
HBM = pl.BlockSpec(memory_space=pltpu.HBM)
SMEM = pl.BlockSpec(memory_space=pltpu.SMEM)
LIMIT = 24 * 1024 * 1024
WHOLE = 63 * 1024 * 1024


def level(step):
    share = step / NSTEPS
    return 5.0 * share / (1.0 + 4.0 * share)


def pack_kernel(q_ref, k_ref, v_ref, out_ref, packed_ref, in_sem, out_sem):
    heads = out_ref.shape[0]
    group = heads // CHUNKS
    for head in range(heads):
        cols = slice(head * HEAD_DIM, (head + 1) * HEAD_DIM)
        for part, ref in enumerate((q_ref, k_ref, v_ref)):
            there = packed_ref.at[head, :, part * HEAD_DIM : (part + 1) * HEAD_DIM]
            pltpu.make_async_copy(ref.at[:, cols], there, in_sem.at[head // group]).start()
    leaving = []
    for chunk in range(CHUNKS):
        mine = packed_ref.at[chunk * group : (chunk + 1) * group]
        pltpu.make_async_copy(mine, mine, in_sem.at[chunk]).wait()
        there = out_ref.at[chunk * group : (chunk + 1) * group]
        leaving.append(pltpu.make_async_copy(mine, there, out_sem.at[chunk]))
        leaving[-1].start()
    for copy in leaving:
        copy.wait()


def pack(queries, keys, values):
    tok, feat = queries.shape
    heads = feat // HEAD_DIM
    shape = (heads, tok, 3 * HEAD_DIM)
    return pl.pallas_call(
        pack_kernel,
        in_specs=[HBM] * 3,
        out_specs=HBM,
        out_shape=jax.ShapeDtypeStruct(shape, queries.dtype),
        scratch_shapes=[
            pltpu.VMEM(shape, queries.dtype),
            pltpu.SemaphoreType.DMA((CHUNKS,)),
            pltpu.SemaphoreType.DMA((CHUNKS,)),
        ],
        compiler_params=pltpu.CompilerParams(vmem_limit_bytes=WHOLE),
    )(queries, keys, values)


def scores_of(q, keys):
    return lax.dot_general(q, keys, (((1,), (1,)), ((), ())), preferred_element_type=jnp.float32)


def frame_of(far):
    odd = lax.rem(lax.axis_index("section"), 2)
    return odd if far else 1 - odd


def own_kernel(qkv_ref, sums_ref, peak_ref, value_ref):
    frame_tok = peak_ref.shape[0]
    first = pl.multiple_of(frame_of(True) * frame_tok, frame_tok)
    own = pl.ds(first, frame_tok)
    value_ref[:, :HEAD_DIM] = qkv_ref[own, 2 * HEAD_DIM :]
    value_ref[:, HEAD_DIM:] = jnp.ones((frame_tok, HEAD_DIM), jnp.bfloat16)
    for index in range(frame_tok // BLOCK):
        rows = pl.ds(index * BLOCK, BLOCK)
        q = qkv_ref[pl.ds(pl.multiple_of(first + index * BLOCK, BLOCK), BLOCK), :HEAD_DIM]
        scores = scores_of(q, qkv_ref[own, HEAD_DIM : 2 * HEAD_DIM])
        peak = jnp.max(scores, axis=-1, keepdims=True)
        weights = jnp.exp2((scores - peak) * SCALE).astype(jnp.bfloat16)
        sums_ref[rows, :] = jnp.dot(weights, value_ref[...], preferred_element_type=jnp.float32)
        peak_ref[rows, :] = jnp.broadcast_to(peak, (BLOCK, HEAD_DIM))


def part_cost(frame_tok):
    return pl.CostEstimate(flops=frame_tok, bytes_accessed=frame_tok, transcendentals=0)


def own_part(qkv):
    frame_tok = qkv.shape[0] // FRAMES
    shapes = [
        jax.ShapeDtypeStruct((frame_tok, 2 * HEAD_DIM), jnp.float32),
        jax.ShapeDtypeStruct((frame_tok, HEAD_DIM), jnp.float32),
    ]
    return pl.pallas_call(
        own_kernel,
        in_specs=[VMEM],
        out_specs=[VMEM] * len(shapes),
        out_shape=shapes,
        scratch_shapes=[pltpu.VMEM((frame_tok, 2 * HEAD_DIM), jnp.bfloat16)],
        compiler_params=pltpu.CompilerParams(vmem_limit_bytes=LIMIT),
        cost_estimate=part_cost(frame_tok),
    )(qkv)


def other_frame(final, far, ws_ref, qkv_ref, halo_ref, key_ref, value_ref):
    frame_tok = qkv_ref.shape[0] // FRAMES
    position = lax.axis_index("section")
    frame = frame_of(far)
    outside = ws_ref[0, frame] == frame - 1
    exists = jnp.where(frame == 0, position > 0, position < final)
    own = pl.ds(pl.multiple_of(frame * frame_tok, frame_tok), frame_tok)
    other = pl.ds(pl.multiple_of((1 - frame) * frame_tok, frame_tok), frame_tok)
    k_cols, v_cols = slice(HEAD_DIM, 2 * HEAD_DIM), slice(2 * HEAD_DIM, 3 * HEAD_DIM)
    value_ref[:, HEAD_DIM:] = jnp.ones((frame_tok, HEAD_DIM), jnp.bfloat16)

    @pl.when(jnp.logical_not(outside))
    def _():
        key_ref[...] = qkv_ref[other, k_cols]
        value_ref[:, :HEAD_DIM] = qkv_ref[other, v_cols]

    @pl.when(jnp.logical_and(outside, exists))
    def _():
        rows = pl.ds(pl.multiple_of((1 - frame) * MORE, MORE), frame_tok) if far else slice(None)
        key_ref[...] = halo_ref[rows, :HEAD_DIM]
        value_ref[:, :HEAD_DIM] = halo_ref[rows, HEAD_DIM:]

    @pl.when(jnp.logical_and(outside, jnp.logical_not(exists)))
    def _():
        key_ref[...] = qkv_ref[own, k_cols]
        value_ref[...] = jnp.zeros((frame_tok, 2 * HEAD_DIM), jnp.bfloat16)


def near_kernel(final, ws_ref, qkv_ref, halo_ref, out_ref, key_ref, value_ref):
    frame_tok = out_ref.shape[0]
    first = pl.multiple_of(frame_of(False) * frame_tok, frame_tok)
    own, rest = pl.ds(first, frame_tok), pl.ds(frame_tok, frame_tok)
    key_ref[:frame_tok] = qkv_ref[own, HEAD_DIM : 2 * HEAD_DIM]
    value_ref[:frame_tok, :HEAD_DIM] = qkv_ref[own, 2 * HEAD_DIM :]
    value_ref[:frame_tok, HEAD_DIM:] = jnp.ones((frame_tok, HEAD_DIM), jnp.bfloat16)
    other_frame(final, False, ws_ref, qkv_ref, halo_ref, key_ref.at[rest], value_ref.at[rest])

    def scores(index):
        rows = pl.ds(pl.multiple_of(first + index * BLOCK, BLOCK), BLOCK)
        return scores_of(qkv_ref[rows, :HEAD_DIM], key_ref[...])

    blocks = frame_tok // BLOCK
    after = scores(0)
    for index in range(blocks):
        here = after
        if index + 1 < blocks:
            after = scores(index + 1)
        peak = jnp.max(here, axis=-1, keepdims=True)
        weights = jnp.exp2((here - peak) * SCALE).astype(jnp.bfloat16)
        sums = jnp.dot(weights, value_ref[...], preferred_element_type=jnp.float32)
        result = (sums[:, :HEAD_DIM] / sums[:, HEAD_DIM:]).astype(jnp.bfloat16)
        out_ref[index * BLOCK : (index + 1) * BLOCK, :] = result


def far_kernel(final, ws_ref, qkv_ref, halo_ref, sums_ref, peak_ref, near_ref, out_ref, key_ref, value_ref, held_ref, sem_ref):
    frame_tok = near_ref.shape[0]
    first = pl.multiple_of(frame_of(True) * frame_tok, frame_tok)
    rest = pl.ds(pl.multiple_of(frame_of(False) * frame_tok, frame_tok), frame_tok)
    copies = [pltpu.make_async_copy(near_ref, out_ref.at[rest], sem_ref.at[0])]
    copies[0].start()
    other_frame(final, True, ws_ref, qkv_ref, halo_ref, key_ref, value_ref)

    def scores(index):
        rows = pl.ds(pl.multiple_of(first + index * BLOCK, BLOCK), BLOCK)
        return scores_of(qkv_ref[rows, :HEAD_DIM], key_ref[...])

    blocks = frame_tok // BLOCK
    after = scores(0)
    for index in range(blocks):
        here = after
        if index + 1 < blocks:
            after = scores(index + 1)
        rows = pl.ds(index * BLOCK, BLOCK)
        before = peak_ref[rows, :]
        peak = jnp.maximum(jnp.broadcast_to(jnp.max(here, axis=-1, keepdims=True), before.shape), before)
        spread = jnp.concatenate([peak] * (frame_tok // HEAD_DIM), axis=1)
        weights = jnp.exp2((here - spread) * SCALE).astype(jnp.bfloat16)
        sums = jnp.dot(weights, value_ref[...], preferred_element_type=jnp.float32)
        share = jnp.exp2((before - peak) * SCALE)
        mixed = sums[:, :HEAD_DIM] + sums_ref[rows, :HEAD_DIM] * share
        total = sums[:, HEAD_DIM:] + sums_ref[rows, HEAD_DIM:] * share
        held_ref[rows, :] = (mixed / total).astype(jnp.bfloat16)
        there = out_ref.at[pl.ds(pl.multiple_of(first + index * BLOCK, BLOCK), BLOCK)]
        copies.append(pltpu.make_async_copy(held_ref.at[rows], there, sem_ref.at[1 + index]))
        copies[-1].start()
    for copy in copies:
        copy.wait()


def window_part(far, final, window_start, qkv, *others):
    frame_tok = qkv.shape[0] // FRAMES
    out = jax.ShapeDtypeStruct((FRAMES * frame_tok if far else frame_tok, HEAD_DIM), qkv.dtype)
    keys = frame_tok if far else FRAMES * frame_tok
    scratch = [pltpu.VMEM((keys, HEAD_DIM), jnp.bfloat16), pltpu.VMEM((keys, 2 * HEAD_DIM), jnp.bfloat16)]
    if far:
        scratch += [pltpu.VMEM((frame_tok, HEAD_DIM), jnp.bfloat16), pltpu.SemaphoreType.DMA((1 + frame_tok // BLOCK,))]
    return pl.pallas_call(
        functools.partial(far_kernel if far else near_kernel, final),
        in_specs=[SMEM] + [VMEM] * (1 + len(others)),
        out_specs=HBM if far else VMEM,
        out_shape=out,
        scratch_shapes=scratch,
        compiler_params=pltpu.CompilerParams(vmem_limit_bytes=LIMIT),
        cost_estimate=part_cost(frame_tok),
    )(window_start, qkv, *others)


def velocity_of(step_ref, att_ref, mod_ref, begin, tok):
    heads = att_ref.shape[0]
    rows = slice(begin, begin + tok)
    squares = jnp.zeros((tok, HEAD_DIM), jnp.float32)
    for head in range(heads):
        a = att_ref[head, rows].astype(jnp.float32)
        squares += a * a
    mean = jnp.sum(squares, axis=-1, keepdims=True) / (heads * HEAD_DIM)
    inverse = jnp.broadcast_to(1.0 / jnp.sqrt(mean + 1e-06), (tok, HEAD_DIM))
    chosen = lax.broadcasted_iota(jnp.int32, (NSTEPS, HEAD_DIM), 0) == step_ref[0]
    for head in range(heads):
        cols = slice(head * HEAD_DIM, (head + 1) * HEAD_DIM)
        gain = jnp.sum(jnp.where(chosen, mod_ref[:, cols], 0.0), axis=0, keepdims=True)
        yield cols, att_ref[head, rows].astype(jnp.float32) * inverse * gain


def update_kernel(final, begin, step_ref, att_ref, mod_ref, state_ref, fresh_ref, passed_ref):
    tok = passed_ref.shape[0]
    rows = slice(begin, begin + tok)
    now = jnp.full((1, HEAD_DIM), step_ref[0], jnp.int32)
    delta = level((now - 1).astype(jnp.float32)) - level(now.astype(jnp.float32))
    for cols, moving in velocity_of(step_ref, att_ref, mod_ref, begin, tok):
        passed_ref[:, cols] = (state_ref[rows, cols].astype(jnp.float32) + delta * moving).astype(jnp.bfloat16)

    @pl.when(lax.axis_index("section") == final)
    def _():
        passed_ref[...] = fresh_ref[rows]


def velocity_kernel(step_ref, att_ref, mod_ref, velocity_ref):
    for cols, moving in velocity_of(step_ref, att_ref, mod_ref, 0, velocity_ref.shape[0]):
        velocity_ref[:, cols] = moving.astype(jnp.bfloat16)


def finish(kernel, tok, timestep, attended, modulation, *others):
    heads = attended.shape[0]
    return pl.pallas_call(
        kernel,
        in_specs=[SMEM] + [VMEM] * (2 + len(others)),
        out_specs=VMEM,
        out_shape=jax.ShapeDtypeStruct((tok, heads * HEAD_DIM), attended.dtype),
        compiler_params=pltpu.CompilerParams(vmem_limit_bytes=LIMIT),
        cost_estimate=pl.CostEstimate(flops=10 * tok * heads * HEAD_DIM, bytes_accessed=6 * tok * heads * HEAD_DIM, transcendentals=0),
    )(timestep, attended, modulation, *others)


def per_device(queries, keys, values, queue_state, fresh_state, timestep, window_start, modulation):
    tok_dev, feat = queries.shape
    sections = lax.axis_size("section")
    frame_tok = tok_dev * lax.axis_size("seq") // FRAMES
    packed = pack(queries, keys, values)
    qkv = lax.all_to_all(packed, "seq", split_axis=0, concat_axis=0, tiled=True)
    qkv = qkv.reshape(FRAMES * frame_tok, 3 * HEAD_DIM)
    start = frame_of(True) * (frame_tok - MORE)
    facing = lax.dynamic_slice(qkv, (start, HEAD_DIM), (frame_tok + MORE, 2 * HEAD_DIM))
    pairs = [(i, i + 1) for i in range(1, sections - 1, 2)]
    far = lax.ppermute(facing, "section", pairs + [(j, i) for i, j in pairs])
    facing = lax.dynamic_slice(qkv, (frame_of(False) * frame_tok, HEAD_DIM), (frame_tok, 2 * HEAD_DIM))
    pairs = [(i, i + 1) for i in range(0, sections - 1, 2)]
    near = lax.ppermute(facing, "section", pairs + [(j, i) for i, j in pairs])
    sums, peak = own_part(qkv)
    near_out = window_part(False, sections - 1, window_start, qkv, near)
    attended = window_part(True, sections - 1, window_start, qkv, far, sums, peak, near_out)
    attended = attended.reshape(feat // HEAD_DIM, tok_dev, HEAD_DIM)
    attended = lax.all_to_all(attended, "seq", split_axis=0, concat_axis=0, tiled=True)
    ring = [(i, (i + 1) % sections) for i in range(sections)]
    half = tok_dev // 2
    halves = []
    for begin in (0, half):
        update = functools.partial(update_kernel, sections - 1, begin)
        passed = finish(update, half, timestep, attended, modulation, queue_state, fresh_state)
        halves.append(lax.ppermute(passed, "section", ring))
    velocity = finish(velocity_kernel, tok_dev, timestep, attended, modulation)
    return velocity, jnp.concatenate(halves, axis=0)


def solution(mesh):
    return jax.shard_map(
        per_device,
        mesh=mesh,
        in_specs=(
            P(("section", "seq"), None),
            P(("section", "seq"), None),
            P(("section", "seq"), None),
            P(("section", "seq"), None),
            P("seq", None),
            P("section"),
            P("section", None),
            P(),
        ),
        out_specs=(P(("section", "seq"), None), P(("section", "seq"), None)),
        check_vma=False,
    )
```

```python
import functools

import jax
import jax.numpy as jnp
from jax import lax
from jax.experimental import pallas as pl
from jax.experimental.pallas import tpu as pltpu
from jax.sharding import PartitionSpec as P

HEAD_DIM = 128
FRAMES = 2
NSTEPS = 16
SCALE = 1.4426950408889634 / HEAD_DIM**0.5
BLOCK = 256
FAR_BLOCK = 512
CHUNKS = 4
MORE = 16
VMEM = pl.BlockSpec(memory_space=pltpu.VMEM)
HBM = pl.BlockSpec(memory_space=pltpu.HBM)
SMEM = pl.BlockSpec(memory_space=pltpu.SMEM)
LIMIT = 24 * 1024 * 1024
WHOLE = 63 * 1024 * 1024


def level(step):
    share = step / NSTEPS
    return 5.0 * share / (1.0 + 4.0 * share)


def pack_kernel(q_ref, k_ref, v_ref, out_ref, packed_ref, in_sem, out_sem):
    heads = out_ref.shape[0]
    group = heads // CHUNKS
    for head in range(heads):
        cols = slice(head * HEAD_DIM, (head + 1) * HEAD_DIM)
        for part, ref in enumerate((q_ref, k_ref, v_ref)):
            there = packed_ref.at[head, :, part * HEAD_DIM : (part + 1) * HEAD_DIM]
            pltpu.make_async_copy(ref.at[:, cols], there, in_sem.at[head // group]).start()
    leaving = []
    for chunk in range(CHUNKS):
        mine = packed_ref.at[chunk * group : (chunk + 1) * group]
        pltpu.make_async_copy(mine, mine, in_sem.at[chunk]).wait()
        there = out_ref.at[chunk * group : (chunk + 1) * group]
        leaving.append(pltpu.make_async_copy(mine, there, out_sem.at[chunk]))
        leaving[-1].start()
    for copy in leaving:
        copy.wait()


def pack(queries, keys, values):
    tok, feat = queries.shape
    heads = feat // HEAD_DIM
    shape = (heads, tok, 3 * HEAD_DIM)
    return pl.pallas_call(
        pack_kernel,
        in_specs=[HBM] * 3,
        out_specs=HBM,
        out_shape=jax.ShapeDtypeStruct(shape, queries.dtype),
        scratch_shapes=[
            pltpu.VMEM(shape, queries.dtype),
            pltpu.SemaphoreType.DMA((CHUNKS,)),
            pltpu.SemaphoreType.DMA((CHUNKS,)),
        ],
        compiler_params=pltpu.CompilerParams(vmem_limit_bytes=WHOLE),
    )(queries, keys, values)


def scores_of(q, keys):
    return lax.dot_general(q, keys, (((1,), (1,)), ((), ())), preferred_element_type=jnp.float32)


def frame_of(far):
    odd = lax.rem(lax.axis_index("section"), 2)
    return odd if far else 1 - odd


def own_kernel(qkv_ref, sums_ref, peak_ref, value_ref):
    frame_tok = peak_ref.shape[0]
    first = pl.multiple_of(frame_of(True) * frame_tok, frame_tok)
    own = pl.ds(first, frame_tok)
    value_ref[:, :HEAD_DIM] = qkv_ref[own, 2 * HEAD_DIM :]
    value_ref[:, HEAD_DIM:] = jnp.ones((frame_tok, HEAD_DIM), jnp.bfloat16)
    for index in range(frame_tok // BLOCK):
        rows = pl.ds(index * BLOCK, BLOCK)
        q = qkv_ref[pl.ds(pl.multiple_of(first + index * BLOCK, BLOCK), BLOCK), :HEAD_DIM]
        scores = scores_of(q, qkv_ref[own, HEAD_DIM : 2 * HEAD_DIM])
        peak = jnp.max(scores, axis=-1, keepdims=True)
        weights = jnp.exp2((scores - peak) * SCALE).astype(jnp.bfloat16)
        sums_ref[rows, :] = jnp.dot(weights, value_ref[...], preferred_element_type=jnp.float32)
        peak_ref[rows, :] = jnp.broadcast_to(peak, (BLOCK, HEAD_DIM))


def part_cost(frame_tok):
    return pl.CostEstimate(flops=frame_tok, bytes_accessed=frame_tok, transcendentals=0)


def own_part(qkv):
    frame_tok = qkv.shape[0] // FRAMES
    shapes = [
        jax.ShapeDtypeStruct((frame_tok, 2 * HEAD_DIM), jnp.float32),
        jax.ShapeDtypeStruct((frame_tok, HEAD_DIM), jnp.float32),
    ]
    return pl.pallas_call(
        own_kernel,
        in_specs=[VMEM],
        out_specs=[VMEM] * len(shapes),
        out_shape=shapes,
        scratch_shapes=[pltpu.VMEM((frame_tok, 2 * HEAD_DIM), jnp.bfloat16)],
        compiler_params=pltpu.CompilerParams(vmem_limit_bytes=LIMIT),
        cost_estimate=part_cost(frame_tok),
    )(qkv)


def other_frame(final, far, ws_ref, qkv_ref, halo_ref, key_ref, value_ref):
    frame_tok = qkv_ref.shape[0] // FRAMES
    position = lax.axis_index("section")
    frame = frame_of(far)
    outside = ws_ref[0, frame] == frame - 1
    exists = jnp.where(frame == 0, position > 0, position < final)
    own = pl.ds(pl.multiple_of(frame * frame_tok, frame_tok), frame_tok)
    other = pl.ds(pl.multiple_of((1 - frame) * frame_tok, frame_tok), frame_tok)
    k_cols, v_cols = slice(HEAD_DIM, 2 * HEAD_DIM), slice(2 * HEAD_DIM, 3 * HEAD_DIM)
    value_ref[:, HEAD_DIM:] = jnp.ones((frame_tok, HEAD_DIM), jnp.bfloat16)

    @pl.when(jnp.logical_not(outside))
    def _():
        key_ref[...] = qkv_ref[other, k_cols]
        value_ref[:, :HEAD_DIM] = qkv_ref[other, v_cols]

    @pl.when(jnp.logical_and(outside, exists))
    def _():
        rows = pl.ds(pl.multiple_of((1 - frame) * MORE, MORE), frame_tok) if far else slice(None)
        key_ref[...] = halo_ref[rows, :HEAD_DIM]
        value_ref[:, :HEAD_DIM] = halo_ref[rows, HEAD_DIM:]

    @pl.when(jnp.logical_and(outside, jnp.logical_not(exists)))
    def _():
        key_ref[...] = qkv_ref[own, k_cols]
        value_ref[...] = jnp.zeros((frame_tok, 2 * HEAD_DIM), jnp.bfloat16)


def near_kernel(final, ws_ref, qkv_ref, halo_ref, out_ref, key_ref, value_ref):
    frame_tok = out_ref.shape[0]
    first = pl.multiple_of(frame_of(False) * frame_tok, frame_tok)
    own, rest = pl.ds(first, frame_tok), pl.ds(frame_tok, frame_tok)
    key_ref[:frame_tok] = qkv_ref[own, HEAD_DIM : 2 * HEAD_DIM]
    value_ref[:frame_tok, :HEAD_DIM] = qkv_ref[own, 2 * HEAD_DIM :]
    value_ref[:frame_tok, HEAD_DIM:] = jnp.ones((frame_tok, HEAD_DIM), jnp.bfloat16)
    other_frame(final, False, ws_ref, qkv_ref, halo_ref, key_ref.at[rest], value_ref.at[rest])

    def scores(index):
        rows = pl.ds(pl.multiple_of(first + index * BLOCK, BLOCK), BLOCK)
        return scores_of(qkv_ref[rows, :HEAD_DIM], key_ref[...])

    blocks = frame_tok // BLOCK
    after = scores(0)
    for index in range(blocks):
        here = after
        if index + 1 < blocks:
            after = scores(index + 1)
        peak = jnp.max(here, axis=-1, keepdims=True)
        weights = jnp.exp2((here - peak) * SCALE).astype(jnp.bfloat16)
        sums = jnp.dot(weights, value_ref[...], preferred_element_type=jnp.float32)
        result = (sums[:, :HEAD_DIM] / sums[:, HEAD_DIM:]).astype(jnp.bfloat16)
        out_ref[index * BLOCK : (index + 1) * BLOCK, :] = result


def far_kernel(final, ws_ref, qkv_ref, halo_ref, sums_ref, peak_ref, near_ref, out_ref, key_ref, value_ref, held_ref, sem_ref):
    frame_tok = near_ref.shape[0]
    first = pl.multiple_of(frame_of(True) * frame_tok, frame_tok)
    rest = pl.ds(pl.multiple_of(frame_of(False) * frame_tok, frame_tok), frame_tok)
    copies = [pltpu.make_async_copy(near_ref, out_ref.at[rest], sem_ref.at[0])]
    copies[0].start()
    other_frame(final, True, ws_ref, qkv_ref, halo_ref, key_ref, value_ref)

    def scores(index):
        rows = pl.ds(pl.multiple_of(first + index * FAR_BLOCK, FAR_BLOCK), FAR_BLOCK)
        return scores_of(qkv_ref[rows, :HEAD_DIM], key_ref[...])

    blocks = frame_tok // FAR_BLOCK
    after = scores(0)
    for index in range(blocks):
        here = after
        if index + 1 < blocks:
            after = scores(index + 1)
        rows = pl.ds(index * FAR_BLOCK, FAR_BLOCK)
        before = peak_ref[rows, :]
        peak = jnp.maximum(jnp.broadcast_to(jnp.max(here, axis=-1, keepdims=True), before.shape), before)
        spread = jnp.concatenate([peak] * (frame_tok // HEAD_DIM), axis=1)
        weights = jnp.exp2((here - spread) * SCALE).astype(jnp.bfloat16)
        sums = jnp.dot(weights, value_ref[...], preferred_element_type=jnp.float32)
        share = jnp.exp2((before - peak) * SCALE)
        mixed = sums[:, :HEAD_DIM] + sums_ref[rows, :HEAD_DIM] * share
        total = sums[:, HEAD_DIM:] + sums_ref[rows, HEAD_DIM:] * share
        held_ref[rows, :] = (mixed / total).astype(jnp.bfloat16)
        there = out_ref.at[pl.ds(pl.multiple_of(first + index * FAR_BLOCK, FAR_BLOCK), FAR_BLOCK)]
        copies.append(pltpu.make_async_copy(held_ref.at[rows], there, sem_ref.at[1 + index]))
        copies[-1].start()
    for copy in copies:
        copy.wait()


def window_part(far, final, window_start, qkv, *others):
    frame_tok = qkv.shape[0] // FRAMES
    out = jax.ShapeDtypeStruct((FRAMES * frame_tok if far else frame_tok, HEAD_DIM), qkv.dtype)
    keys = frame_tok if far else FRAMES * frame_tok
    scratch = [pltpu.VMEM((keys, HEAD_DIM), jnp.bfloat16), pltpu.VMEM((keys, 2 * HEAD_DIM), jnp.bfloat16)]
    if far:
        scratch += [pltpu.VMEM((frame_tok, HEAD_DIM), jnp.bfloat16), pltpu.SemaphoreType.DMA((1 + frame_tok // FAR_BLOCK,))]
    return pl.pallas_call(
        functools.partial(far_kernel if far else near_kernel, final),
        in_specs=[SMEM] + [VMEM] * (1 + len(others)),
        out_specs=HBM if far else VMEM,
        out_shape=out,
        scratch_shapes=scratch,
        compiler_params=pltpu.CompilerParams(vmem_limit_bytes=LIMIT),
        cost_estimate=part_cost(frame_tok),
    )(window_start, qkv, *others)


def velocity_of(step_ref, att_ref, mod_ref):
    heads, tok, _ = att_ref.shape
    squares = jnp.zeros((tok, HEAD_DIM), jnp.float32)
    for head in range(heads):
        a = att_ref[head].astype(jnp.float32)
        squares += a * a
    mean = jnp.sum(squares, axis=-1, keepdims=True) / (heads * HEAD_DIM)
    inverse = jnp.broadcast_to(1.0 / jnp.sqrt(mean + 1e-06), (tok, HEAD_DIM))
    chosen = lax.broadcasted_iota(jnp.int32, (NSTEPS, HEAD_DIM), 0) == step_ref[0]
    for head in range(heads):
        cols = slice(head * HEAD_DIM, (head + 1) * HEAD_DIM)
        gain = jnp.sum(jnp.where(chosen, mod_ref[:, cols], 0.0), axis=0, keepdims=True)
        yield cols, att_ref[head].astype(jnp.float32) * inverse * gain


def update_kernel(final, step_ref, att_ref, mod_ref, state_ref, fresh_ref, passed_ref):
    now = jnp.full((1, HEAD_DIM), step_ref[0], jnp.int32)
    delta = level((now - 1).astype(jnp.float32)) - level(now.astype(jnp.float32))
    for cols, moving in velocity_of(step_ref, att_ref, mod_ref):
        passed_ref[:, cols] = (state_ref[:, cols].astype(jnp.float32) + delta * moving).astype(jnp.bfloat16)

    @pl.when(lax.axis_index("section") == final)
    def _():
        passed_ref[...] = fresh_ref[...]


def velocity_kernel(step_ref, att_ref, mod_ref, velocity_ref):
    for cols, moving in velocity_of(step_ref, att_ref, mod_ref):
        velocity_ref[:, cols] = moving.astype(jnp.bfloat16)


def finish(kernel, timestep, attended, modulation, *others):
    heads, tok, _ = attended.shape
    return pl.pallas_call(
        kernel,
        in_specs=[SMEM] + [VMEM] * (2 + len(others)),
        out_specs=VMEM,
        out_shape=jax.ShapeDtypeStruct((tok, heads * HEAD_DIM), attended.dtype),
        compiler_params=pltpu.CompilerParams(vmem_limit_bytes=LIMIT),
        cost_estimate=pl.CostEstimate(flops=10 * tok * heads * HEAD_DIM, bytes_accessed=6 * tok * heads * HEAD_DIM, transcendentals=0),
    )(timestep, attended, modulation, *others)


def per_device(queries, keys, values, queue_state, fresh_state, timestep, window_start, modulation):
    tok_dev, feat = queries.shape
    sections = lax.axis_size("section")
    frame_tok = tok_dev * lax.axis_size("seq") // FRAMES
    packed = pack(queries, keys, values)
    qkv = lax.all_to_all(packed, "seq", split_axis=0, concat_axis=0, tiled=True)
    qkv = qkv.reshape(FRAMES * frame_tok, 3 * HEAD_DIM)
    start = frame_of(True) * (frame_tok - MORE)
    facing = lax.dynamic_slice(qkv, (start, HEAD_DIM), (frame_tok + MORE, 2 * HEAD_DIM))
    pairs = [(i, i + 1) for i in range(1, sections - 1, 2)]
    far = lax.ppermute(facing, "section", pairs + [(j, i) for i, j in pairs])
    facing = lax.dynamic_slice(qkv, (frame_of(False) * frame_tok, HEAD_DIM), (frame_tok, 2 * HEAD_DIM))
    pairs = [(i, i + 1) for i in range(0, sections - 1, 2)]
    near = lax.ppermute(facing, "section", pairs + [(j, i) for i, j in pairs])
    sums, peak = own_part(qkv)
    near_out = window_part(False, sections - 1, window_start, qkv, near)
    attended = window_part(True, sections - 1, window_start, qkv, far, sums, peak, near_out)
    attended = attended.reshape(feat // HEAD_DIM, tok_dev, HEAD_DIM)
    attended = lax.all_to_all(attended, "seq", split_axis=0, concat_axis=0, tiled=True)
    update = functools.partial(update_kernel, sections - 1)
    passed = finish(update, timestep, attended, modulation, queue_state, fresh_state)
    advanced = lax.ppermute(passed, "section", [(i, (i + 1) % sections) for i in range(sections)])
    velocity = finish(velocity_kernel, timestep, attended, modulation)
    return velocity, advanced


def solution(mesh):
    return jax.shard_map(
        per_device,
        mesh=mesh,
        in_specs=(
            P(("section", "seq"), None),
            P(("section", "seq"), None),
            P(("section", "seq"), None),
            P(("section", "seq"), None),
            P("seq", None),
            P("section"),
            P("section", None),
            P(),
        ),
        out_specs=(P(("section", "seq"), None), P(("section", "seq"), None)),
        check_vma=False,
    )
```

```python
import functools

import jax
import jax.numpy as jnp
from jax import lax
from jax.experimental import pallas as pl
from jax.experimental.pallas import tpu as pltpu
from jax.sharding import PartitionSpec as P

HEAD_DIM = 128
FRAMES = 2
NSTEPS = 16
SCALE = 1.4426950408889634 / HEAD_DIM**0.5
BLOCK = 256
CHUNKS = 4
MORE = 16
VMEM = pl.BlockSpec(memory_space=pltpu.VMEM)
HBM = pl.BlockSpec(memory_space=pltpu.HBM)
SMEM = pl.BlockSpec(memory_space=pltpu.SMEM)
LIMIT = 24 * 1024 * 1024
WHOLE = 63 * 1024 * 1024


def level(step):
    share = step / NSTEPS
    return 5.0 * share / (1.0 + 4.0 * share)


def pack_kernel(q_ref, k_ref, v_ref, out_ref, packed_ref, in_sem, out_sem):
    heads = out_ref.shape[0]
    group = heads // CHUNKS
    for head in range(heads):
        cols = slice(head * HEAD_DIM, (head + 1) * HEAD_DIM)
        for part, ref in enumerate((q_ref, k_ref, v_ref)):
            there = packed_ref.at[head, :, part * HEAD_DIM : (part + 1) * HEAD_DIM]
            pltpu.make_async_copy(ref.at[:, cols], there, in_sem.at[head // group]).start()
    leaving = []
    for chunk in range(CHUNKS):
        mine = packed_ref.at[chunk * group : (chunk + 1) * group]
        pltpu.make_async_copy(mine, mine, in_sem.at[chunk]).wait()
        there = out_ref.at[chunk * group : (chunk + 1) * group]
        leaving.append(pltpu.make_async_copy(mine, there, out_sem.at[chunk]))
        leaving[-1].start()
    for copy in leaving:
        copy.wait()


def pack(queries, keys, values):
    tok, feat = queries.shape
    heads = feat // HEAD_DIM
    shape = (heads, tok, 3 * HEAD_DIM)
    return pl.pallas_call(
        pack_kernel,
        in_specs=[HBM] * 3,
        out_specs=HBM,
        out_shape=jax.ShapeDtypeStruct(shape, queries.dtype),
        scratch_shapes=[
            pltpu.VMEM(shape, queries.dtype),
            pltpu.SemaphoreType.DMA((CHUNKS,)),
            pltpu.SemaphoreType.DMA((CHUNKS,)),
        ],
        compiler_params=pltpu.CompilerParams(vmem_limit_bytes=WHOLE),
    )(queries, keys, values)


def scores_of(q, keys):
    return lax.dot_general(q, keys, (((1,), (1,)), ((), ())), preferred_element_type=jnp.float32)


def frame_of(far):
    odd = lax.rem(lax.axis_index("section"), 2)
    return odd if far else 1 - odd


def own_kernel(qkv_ref, sums_ref, peak_ref, value_ref):
    frame_tok = peak_ref.shape[0]
    first = pl.multiple_of(frame_of(True) * frame_tok, frame_tok)
    own = pl.ds(first, frame_tok)
    value_ref[:, :HEAD_DIM] = qkv_ref[own, 2 * HEAD_DIM :]
    value_ref[:, HEAD_DIM:] = jnp.ones((frame_tok, HEAD_DIM), jnp.bfloat16)
    for index in range(frame_tok // BLOCK):
        rows = pl.ds(index * BLOCK, BLOCK)
        q = qkv_ref[pl.ds(pl.multiple_of(first + index * BLOCK, BLOCK), BLOCK), :HEAD_DIM]
        scores = scores_of(q, qkv_ref[own, HEAD_DIM : 2 * HEAD_DIM])
        peak = jnp.max(scores, axis=-1, keepdims=True)
        weights = jnp.exp2((scores - peak) * SCALE).astype(jnp.bfloat16)
        sums_ref[rows, :] = jnp.dot(weights, value_ref[...], preferred_element_type=jnp.float32)
        peak_ref[rows, :] = jnp.broadcast_to(peak, (BLOCK, HEAD_DIM))


def part_cost(frame_tok):
    return pl.CostEstimate(flops=frame_tok, bytes_accessed=frame_tok, transcendentals=0)


def own_part(qkv):
    frame_tok = qkv.shape[0] // FRAMES
    shapes = [
        jax.ShapeDtypeStruct((frame_tok, 2 * HEAD_DIM), jnp.float32),
        jax.ShapeDtypeStruct((frame_tok, HEAD_DIM), jnp.float32),
    ]
    return pl.pallas_call(
        own_kernel,
        in_specs=[VMEM],
        out_specs=[VMEM] * len(shapes),
        out_shape=shapes,
        scratch_shapes=[pltpu.VMEM((frame_tok, 2 * HEAD_DIM), jnp.bfloat16)],
        compiler_params=pltpu.CompilerParams(vmem_limit_bytes=LIMIT),
        cost_estimate=part_cost(frame_tok),
    )(qkv)


def other_frame(final, far, ws_ref, qkv_ref, halo_ref, key_ref, value_ref):
    frame_tok = qkv_ref.shape[0] // FRAMES
    position = lax.axis_index("section")
    frame = frame_of(far)
    outside = ws_ref[0, frame] == frame - 1
    exists = jnp.where(frame == 0, position > 0, position < final)
    own = pl.ds(pl.multiple_of(frame * frame_tok, frame_tok), frame_tok)
    other = pl.ds(pl.multiple_of((1 - frame) * frame_tok, frame_tok), frame_tok)
    k_cols, v_cols = slice(HEAD_DIM, 2 * HEAD_DIM), slice(2 * HEAD_DIM, 3 * HEAD_DIM)
    value_ref[:, HEAD_DIM:] = jnp.ones((frame_tok, HEAD_DIM), jnp.bfloat16)

    @pl.when(jnp.logical_not(outside))
    def _():
        key_ref[...] = qkv_ref[other, k_cols]
        value_ref[:, :HEAD_DIM] = qkv_ref[other, v_cols]

    @pl.when(jnp.logical_and(outside, exists))
    def _():
        rows = pl.ds(pl.multiple_of((1 - frame) * MORE, MORE), frame_tok) if far else slice(None)
        key_ref[...] = halo_ref[rows, :HEAD_DIM]
        value_ref[:, :HEAD_DIM] = halo_ref[rows, HEAD_DIM:]

    @pl.when(jnp.logical_and(outside, jnp.logical_not(exists)))
    def _():
        key_ref[...] = qkv_ref[own, k_cols]
        value_ref[...] = jnp.zeros((frame_tok, 2 * HEAD_DIM), jnp.bfloat16)


def near_kernel(final, ws_ref, qkv_ref, halo_ref, out_ref, key_ref, value_ref):
    frame_tok = out_ref.shape[0]
    first = pl.multiple_of(frame_of(False) * frame_tok, frame_tok)
    own, rest = pl.ds(first, frame_tok), pl.ds(frame_tok, frame_tok)
    key_ref[:frame_tok] = qkv_ref[own, HEAD_DIM : 2 * HEAD_DIM]
    value_ref[:frame_tok, :HEAD_DIM] = qkv_ref[own, 2 * HEAD_DIM :]
    value_ref[:frame_tok, HEAD_DIM:] = jnp.ones((frame_tok, HEAD_DIM), jnp.bfloat16)
    other_frame(final, False, ws_ref, qkv_ref, halo_ref, key_ref.at[rest], value_ref.at[rest])

    def scores(index):
        rows = pl.ds(pl.multiple_of(first + index * BLOCK, BLOCK), BLOCK)
        return scores_of(qkv_ref[rows, :HEAD_DIM], key_ref[...])

    blocks = frame_tok // BLOCK
    after = scores(0)
    for index in range(blocks):
        here = after
        if index + 1 < blocks:
            after = scores(index + 1)
        peak = jnp.max(here, axis=-1, keepdims=True)
        weights = jnp.exp2((here - peak) * SCALE).astype(jnp.bfloat16)
        sums = jnp.dot(weights, value_ref[...], preferred_element_type=jnp.float32)
        result = (sums[:, :HEAD_DIM] / sums[:, HEAD_DIM:]).astype(jnp.bfloat16)
        out_ref[index * BLOCK : (index + 1) * BLOCK, :] = result


def far_kernel(final, ws_ref, qkv_ref, halo_ref, sums_ref, peak_ref, near_ref, out_ref, key_ref, value_ref, held_ref, sem_ref):
    frame_tok = near_ref.shape[0]
    first = pl.multiple_of(frame_of(True) * frame_tok, frame_tok)
    rest = pl.ds(pl.multiple_of(frame_of(False) * frame_tok, frame_tok), frame_tok)
    copies = [pltpu.make_async_copy(near_ref, out_ref.at[rest], sem_ref.at[0])]
    copies[0].start()
    other_frame(final, True, ws_ref, qkv_ref, halo_ref, key_ref, value_ref)

    def scores(index):
        rows = pl.ds(pl.multiple_of(first + index * BLOCK, BLOCK), BLOCK)
        return scores_of(qkv_ref[rows, :HEAD_DIM], key_ref[...])

    blocks = frame_tok // BLOCK
    after = scores(0)
    for index in range(blocks):
        here = after
        if index + 1 < blocks:
            after = scores(index + 1)
        rows = pl.ds(index * BLOCK, BLOCK)
        before = peak_ref[rows, :]
        peak = jnp.maximum(jnp.broadcast_to(jnp.max(here, axis=-1, keepdims=True), before.shape), before)
        spread = jnp.concatenate([peak] * (frame_tok // HEAD_DIM), axis=1)
        weights = jnp.exp2((here - spread) * SCALE).astype(jnp.bfloat16)
        sums = jnp.dot(weights, value_ref[...], preferred_element_type=jnp.float32)
        share = jnp.exp2((before - peak) * SCALE)
        mixed = sums[:, :HEAD_DIM] + sums_ref[rows, :HEAD_DIM] * share
        total = sums[:, HEAD_DIM:] + sums_ref[rows, HEAD_DIM:] * share
        held_ref[rows, :] = (mixed / total).astype(jnp.bfloat16)
        there = out_ref.at[pl.ds(pl.multiple_of(first + index * BLOCK, BLOCK), BLOCK)]
        copies.append(pltpu.make_async_copy(held_ref.at[rows], there, sem_ref.at[1 + index]))
        copies[-1].start()
    for copy in copies:
        copy.wait()


def window_part(far, final, window_start, qkv, *others):
    frame_tok = qkv.shape[0] // FRAMES
    out = jax.ShapeDtypeStruct((FRAMES * frame_tok if far else frame_tok, HEAD_DIM), qkv.dtype)
    keys = frame_tok if far else FRAMES * frame_tok
    scratch = [pltpu.VMEM((keys, HEAD_DIM), jnp.bfloat16), pltpu.VMEM((keys, 2 * HEAD_DIM), jnp.bfloat16)]
    if far:
        scratch += [pltpu.VMEM((frame_tok, HEAD_DIM), jnp.bfloat16), pltpu.SemaphoreType.DMA((1 + frame_tok // BLOCK,))]
    return pl.pallas_call(
        functools.partial(far_kernel if far else near_kernel, final),
        in_specs=[SMEM] + [VMEM] * (1 + len(others)),
        out_specs=HBM if far else VMEM,
        out_shape=out,
        scratch_shapes=scratch,
        compiler_params=pltpu.CompilerParams(vmem_limit_bytes=LIMIT),
        cost_estimate=part_cost(frame_tok),
    )(window_start, qkv, *others)


def velocity_of(att_ref, gain_ref):
    heads, tok, _ = att_ref.shape
    squares = jnp.zeros((tok, HEAD_DIM), jnp.float32)
    for head in range(heads):
        a = att_ref[head].astype(jnp.float32)
        squares += a * a
    mean = jnp.sum(squares, axis=-1, keepdims=True) / (heads * HEAD_DIM)
    inverse = jnp.broadcast_to(1.0 / jnp.sqrt(mean + 1e-06), (tok, HEAD_DIM))
    for head in range(heads):
        cols = slice(head * HEAD_DIM, (head + 1) * HEAD_DIM)
        yield cols, att_ref[head].astype(jnp.float32) * inverse * gain_ref[:1, cols]


def update_kernel(final, step_ref, att_ref, gain_ref, state_ref, fresh_ref, passed_ref):
    now = jnp.full((1, HEAD_DIM), step_ref[0], jnp.int32)
    delta = level((now - 1).astype(jnp.float32)) - level(now.astype(jnp.float32))
    for cols, moving in velocity_of(att_ref, gain_ref):
        passed_ref[:, cols] = (state_ref[:, cols].astype(jnp.float32) + delta * moving).astype(jnp.bfloat16)

    @pl.when(lax.axis_index("section") == final)
    def _():
        passed_ref[...] = fresh_ref[...]


def velocity_kernel(step_ref, att_ref, gain_ref, velocity_ref):
    for cols, moving in velocity_of(att_ref, gain_ref):
        velocity_ref[:, cols] = moving.astype(jnp.bfloat16)


def gain_kernel(step_ref, mod_ref, gain_ref):
    chosen = lax.broadcasted_iota(jnp.int32, mod_ref.shape, 0) == step_ref[0]
    row = jnp.sum(jnp.where(chosen, mod_ref[...], 0.0), axis=0, keepdims=True)
    gain_ref[...] = jnp.broadcast_to(row, gain_ref.shape)


def gain_of(timestep, modulation):
    return pl.pallas_call(
        gain_kernel,
        in_specs=[SMEM, VMEM],
        out_specs=VMEM,
        out_shape=jax.ShapeDtypeStruct((8, modulation.shape[1]), modulation.dtype),
    )(timestep, modulation)


def finish(kernel, timestep, attended, modulation, *others):
    heads, tok, _ = attended.shape
    return pl.pallas_call(
        kernel,
        in_specs=[SMEM] + [VMEM] * (2 + len(others)),
        out_specs=VMEM,
        out_shape=jax.ShapeDtypeStruct((tok, heads * HEAD_DIM), attended.dtype),
        compiler_params=pltpu.CompilerParams(vmem_limit_bytes=LIMIT),
        cost_estimate=pl.CostEstimate(flops=10 * tok * heads * HEAD_DIM, bytes_accessed=6 * tok * heads * HEAD_DIM, transcendentals=0),
    )(timestep, attended, modulation, *others)


def per_device(queries, keys, values, queue_state, fresh_state, timestep, window_start, modulation):
    tok_dev, feat = queries.shape
    sections = lax.axis_size("section")
    frame_tok = tok_dev * lax.axis_size("seq") // FRAMES
    packed = pack(queries, keys, values)
    qkv = lax.all_to_all(packed, "seq", split_axis=0, concat_axis=0, tiled=True)
    qkv = qkv.reshape(FRAMES * frame_tok, 3 * HEAD_DIM)
    start = frame_of(True) * (frame_tok - MORE)
    facing = lax.dynamic_slice(qkv, (start, HEAD_DIM), (frame_tok + MORE, 2 * HEAD_DIM))
    pairs = [(i, i + 1) for i in range(1, sections - 1, 2)]
    far = lax.ppermute(facing, "section", pairs + [(j, i) for i, j in pairs])
    facing = lax.dynamic_slice(qkv, (frame_of(False) * frame_tok, HEAD_DIM), (frame_tok, 2 * HEAD_DIM))
    pairs = [(i, i + 1) for i in range(0, sections - 1, 2)]
    near = lax.ppermute(facing, "section", pairs + [(j, i) for i, j in pairs])
    sums, peak = own_part(qkv)
    near_out = window_part(False, sections - 1, window_start, qkv, near)
    attended = window_part(True, sections - 1, window_start, qkv, far, sums, peak, near_out)
    attended = attended.reshape(feat // HEAD_DIM, tok_dev, HEAD_DIM)
    attended = lax.all_to_all(attended, "seq", split_axis=0, concat_axis=0, tiled=True)
    gain = gain_of(timestep, modulation)
    update = functools.partial(update_kernel, sections - 1)
    passed = finish(update, timestep, attended, gain, queue_state, fresh_state)
    advanced = lax.ppermute(passed, "section", [(i, (i + 1) % sections) for i in range(sections)])
    velocity = finish(velocity_kernel, timestep, attended, gain)
    return velocity, advanced


def solution(mesh):
    return jax.shard_map(
        per_device,
        mesh=mesh,
        in_specs=(
            P(("section", "seq"), None),
            P(("section", "seq"), None),
            P(("section", "seq"), None),
            P(("section", "seq"), None),
            P("seq", None),
            P("section"),
            P("section", None),
            P(),
        ),
        out_specs=(P(("section", "seq"), None), P(("section", "seq"), None)),
        check_vma=False,
    )
```
